256 devices in a mesh: chan: 32 (over y_lo, z, core), tm: 8 (over y_hi, x).
Axes of the slice: x: 4, y: 4 (y_hi: 2, y_lo: 2; y = y_hi * 2 + y_lo), z: 8, core: 2. Of those that a mesh axis runs over, the one named last changes fastest.
Arguments:
- seismic: bfloat16 [3072, 32768], P('chan', 'tm'), may hold values from -180 to 180, as said below
- waveforms: float32 [32, 30, 300], P('chan'), may hold values from -0.5 to 1.5
- channel_list: int32 [32, 30], replicated, may hold values from 0 to 3071, as said below
- moveouts: int32 [32, 30], replicated, may hold values from 0 to 127
Outputs:
- stack: float32 [32, 32768], P('chan', 'tm')
- peaks: float32 [32], P('chan')
The draws below stay inside these ranges and needn't reach their ends.
Inputs may be any that keep to these rules, and one draw needn't show every extreme that they name: `channel_list`: each template lists the three channels 3 s, 3 s + 1, 3 s + 2 of 10 stations s, station by station; no channel appears twice in the whole array; the first and the last channel are always listed. Of the groups of 96 consecutive channels, a quarter hold 60 listed channels, a quarter 3 * 10, and the other half 3 * 5; which groups is drawn. `seismic`: channels differ in gain, and the amplitude varies along time.
All inputs are finite; a program needn't handle non-finite values.
Results may differ from the reference program's by a relative error of at most 0.0029.
Values may be sent and summed in bfloat16 or wider, within the bound.
A program may use at most 128 MiB of HBM per device.

```python
import math
import jax
import jax.numpy as jnp
from jax import lax

CH_DEV = 96
CHANNEL_TOTAL = 3072
RECORD_SAMPLES = 32768
LEN = 300
MOVE = 128
STA_TPL = 10
TPL_CH = 30
TPL_DEV = 1
TEMPLATES = 32


def draw_seismic(key, part):
    key = jax.random.fold_in(key, 11)
    key_background_noise, key_channel_gain, key_pulse_random = jax.random.split(key, 3)
    noise = jnp.clip(jax.random.normal(key_background_noise, (CHANNEL_TOTAL, RECORD_SAMPLES), jnp.float32), -5.0, 5.0)
    gains = jnp.exp(jax.random.uniform(key_channel_gain, (CHANNEL_TOTAL, 1), jnp.float32, 0.0, math.log(10.0)))
    signal_pulses = jnp.exp(jax.random.uniform(key_pulse_random, (CHANNEL_TOTAL, RECORD_SAMPLES // 64), jnp.float32, math.log(0.3), math.log(3.0)))
    amplitude_envelope = jnp.repeat(signal_pulses, 64, axis=1)
    return (noise * gains * amplitude_envelope).astype(jnp.bfloat16)


def lead_with(order, first):
    position = jnp.argmax((order == first).astype(jnp.int32))
    return jnp.roll(order, -position)


def draw_channel_list(key, part):
    key = jax.random.fold_in(key, 23)
    key_rank, key_order, key_mix = jax.random.split(key, 3)
    group_count = CHANNEL_TOTAL // CH_DEV
    per_group = CH_DEV // 3
    mean_load = STA_TPL * TPL_DEV
    ranking = jax.random.permutation(key_rank, group_count)
    loading = jnp.where(ranking < group_count // 4, 2 * mean_load, jnp.where(ranking < group_count // 2, mean_load, mean_load // 2))
    group_keys = jax.random.split(key_order, group_count)
    orders = jax.vmap(lambda sub_key: jax.random.permutation(sub_key, per_group))(group_keys).astype(jnp.int32)
    group_ids = jnp.arange(group_count, dtype=jnp.int32)
    firsts = jnp.where(group_ids == 0, 0, jnp.where(group_ids == group_count - 1, per_group - 1, orders[:, 0])).astype(jnp.int32)
    orders = jax.vmap(lead_with)(orders, firsts)
    station = group_ids[:, None] * per_group + orders
    chosen = (jnp.arange(per_group, dtype=jnp.int32)[None, :] < loading[:, None]).astype(jnp.int32)
    flat_station = station.reshape(-1)
    ordering = jnp.argsort(1 - chosen.reshape(-1), stable=True)[:group_count * mean_load]
    picked = flat_station[ordering]
    picked = picked[jax.random.permutation(key_mix, group_count * mean_load)]
    stations = picked.reshape(TEMPLATES, STA_TPL)
    channels = stations[:, :, None] * 3 + jnp.arange(3, dtype=jnp.int32)[None, None, :]
    return channels.reshape(TEMPLATES, TPL_CH).astype(jnp.int32)


def touch_ends(values, rng, least, high):
    longest = values.shape.index(max(values.shape))
    spots = []
    for shift in (0, 1):
        where = [jax.random.randint(jax.random.fold_in(rng, axis), (), 0, length) for axis, length in enumerate(values.shape)]
        where[longest] = (where[longest] + shift) % values.shape[longest]
        spots.append(tuple(where))
    return values.at[spots[0]].set(least).at[spots[1]].set(high)


def level_of(own_key, shape, shards, low, top_value):
    loudness, own = 1.0, jax.random.fold_in(own_key, 6)
    for axis_at, shards_of in shards:
        draws = jnp.exp(jax.random.uniform(jax.random.fold_in(own, axis_at), (shards_of,), jnp.float32, low / len(shards), top_value / len(shards)))
        loudness = loudness * jnp.repeat(draws, shape[axis_at] // shards_of).reshape([-1 if axis == axis_at else 1 for axis in range(len(shape))])
    return loudness


def setup_inputs(seed: int = 0) -> dict:
    keys = jax.random.split(jax.random.key(seed), 5)
    seismic = draw_seismic(jax.random.fold_in(keys[4], 71), 0)
    waveforms = jnp.clip(-0.5 + 2.0 * jax.random.uniform(keys[1], (TEMPLATES, TPL_CH, LEN), jnp.float32) ** level_of(keys[1], (TEMPLATES, TPL_CH, LEN), ((0, 32),), -0.2, 0.2), -0.5, 1.5)
    channel_list = draw_channel_list(jax.random.fold_in(keys[4], 71), 0)
    moveouts = touch_ends(jax.random.randint(keys[3], (TEMPLATES, TPL_CH), 0, MOVE), jax.random.fold_in(keys[3], 1), 0, MOVE - 1).astype(jnp.int32)
    return {"seismic": seismic, "waveforms": waveforms, "channel_list": channel_list, "moveouts": moveouts}


eps_value = 1e-05

def normalize(waves):
    centered = waves - lax.optimization_barrier(jnp.mean(waves, axis=-1, keepdims=True))
    factor = lax.rsqrt(lax.optimization_barrier(jnp.mean(centered * centered, axis=-1, keepdims=True)) + eps_value) / math.sqrt(waves.shape[-1])
    return (centered * factor).astype(jnp.bfloat16)

def grouped_conv(channel_rows, kernel):
    result = lax.conv_general_dilated(channel_rows[None], kernel, (1,), 'VALID', feature_group_count=channel_rows.shape[0], dimension_numbers=('NCH', 'OIH', 'NCH'), precision=lax.Precision.HIGHEST)
    return result[0]

def moved_row(series, offset):
    return lax.dynamic_slice_in_dim(series, offset, RECORD_SAMPLES)

def reference(seismic, waveforms, channel_list, moveouts):
    normed = normalize(waveforms).astype(jnp.float32)
    extra = MOVE + LEN - 1
    window = jnp.ones((TPL_CH, 1, LEN), jnp.float32)

    def per_template(template_index):
        channel_rows = jnp.take(seismic, channel_list[template_index], axis=0).astype(jnp.float32)
        channel_rows = jnp.pad(channel_rows, ((0, 0), (0, extra)))
        numer = grouped_conv(channel_rows, normed[template_index][:, None, :])
        energy = grouped_conv(channel_rows * channel_rows, window)
        corr = numer * lax.rsqrt(energy / LEN + eps_value) / math.sqrt(LEN)
        shifted = jax.vmap(moved_row)(corr, moveouts[template_index])
        return lax.optimization_barrier(jnp.sum(shifted, axis=0))
    stack = lax.map(per_template, jnp.arange(TEMPLATES, dtype=jnp.int32))
    peaks = lax.optimization_barrier(jnp.max(jnp.abs(stack), axis=1))
    return (stack, peaks)
```

```python
import functools
import math

import jax
import jax.numpy as jnp
from jax import lax
from jax.experimental import pallas as pl
from jax.experimental.pallas import tpu as pltpu
from jax.sharding import PartitionSpec as P

LANES = 128
STATIONS = 20
PER = 3
SLOTS = STATIONS * PER
SEL = 64
HALO = 4
BLOCKS = 4
WAVE_BLOCKS = 3
HALVES = 2
EPS = 1e-05
MESH = pl.DeviceIdType.MESH


def each(count, body):
    def step(i, carry):
        body(i)
        return carry

    lax.fori_loop(0, count, step, 0)


def kernel(
    n_chan, n_tm, length,
    tab, seis, waves,
    stack_out, peak_out,
    x_in, halo_in, rows, turned, lhs, scale, band,
    normed, part_in, part_all, chosen, chosen_in, chosen_all,
    running, outgoing, incoming, peak_mine, peak_in,
    sems, in_sem,
):
    me = lax.axis_index("chan")
    now = lax.axis_index("tm")
    tiles = stack_out.shape[0]
    channels = x_in.shape[0]
    pitch = rows.shape[1]
    flat_rows = rows.reshape(channels * pitch, LANES)
    f32, bf16 = jnp.float32, jnp.bfloat16

    def wait_for(ref, blocks, sem):
        span = ref.at[pl.ds(0, blocks)]
        pltpu.make_async_copy(span, span, sem).wait()

    def chan_peer(d):
        return lax.rem(me + d, n_chan)

    def tm_peer(d):
        return lax.rem(now + d, n_tm)

    barrier = pltpu.get_barrier_semaphore()

    def greet_chan(i):
        pl.semaphore_signal(barrier, inc=1, device_id=(chan_peer(i + 1), now), device_id_type=MESH)

    def greet_tm(i):
        pl.semaphore_signal(barrier, inc=1, device_id=(me, tm_peer(i + 1)), device_id_type=MESH)

    each(n_tm - 1, greet_tm)
    each(n_chan - 1, greet_chan)
    load = pltpu.make_async_copy(seis, x_in, in_sem)
    load.start()

    w = waves[0]
    centered = w - jnp.mean(w, axis=-1, keepdims=True)
    factor = lax.rsqrt(jnp.mean(centered * centered, axis=-1, keepdims=True) + EPS) / math.sqrt(length)
    normed[...] = jnp.zeros_like(normed)
    normed[0 : w.shape[0], 0:length] = (centered * factor).astype(bf16)

    lag = lax.broadcasted_iota(jnp.int32, band.shape, 0) - lax.broadcasted_iota(jnp.int32, band.shape, 1)
    band[...] = jnp.where((lag >= 0) & (lag < length), 1.0, 0.0).astype(bf16)

    load.wait()
    pl.semaphore_wait(barrier, n_chan - 1 + n_tm - 1)

    halo = pltpu.make_async_remote_copy(
        src_ref=x_in.at[:, pl.ds(0, HALO * LANES)], dst_ref=halo_in,
        send_sem=sems.at[0], recv_sem=sems.at[1],
        device_id=(me, jnp.maximum(now - 1, 0)), device_id_type=MESH,
    )

    @pl.when(now > 0)
    def _():
        halo.start()

    sends_part = now < WAVE_BLOCKS * HALVES
    half_of = lax.rem(now, HALVES)
    block_of = jnp.minimum(now // HALVES, WAVE_BLOCKS - 1)
    part = normed.at[pl.ds(half_of * 16, 16), pl.ds(block_of * LANES, LANES)]

    def part_copy(i):
        return pltpu.make_async_remote_copy(
            src_ref=part, dst_ref=part_in.at[me],
            send_sem=sems.at[2], recv_sem=sems.at[3],
            device_id=(chan_peer(i + 1), now), device_id_type=MESH,
        )

    @pl.when(sends_part)
    def _():
        each(n_chan - 1, lambda i: part_copy(i).start())

    def lay(ref, first):
        for i in range(ref.shape[1] // LANES):
            for c in range(0, channels, 16):
                flat_rows[pl.ds(c * pitch + first + i, 16, stride=pitch), :] = ref[
                    c : c + 16, i * LANES : (i + 1) * LANES
                ].astype(f32)

    lay(x_in, 0)

    @pl.when(now < n_tm - 1)
    def _():
        halo.wait_recv()

    @pl.when(now == n_tm - 1)
    def _():
        halo_in[...] = jnp.zeros_like(halo_in)

    lay(halo_in, tiles)

    def chosen_copy(i):
        return pltpu.make_async_remote_copy(
            src_ref=chosen, dst_ref=chosen_in.at[now],
            send_sem=sems.at[4], recv_sem=sems.at[5],
            device_id=(me, tm_peer(i + 1)), device_id_type=MESH,
        )

    @pl.when(sends_part)
    def _():
        wait_for(part_in, n_chan - 1, sems.at[3])
        part_all[pl.ds(me * 16, 16), :] = part[...].astype(f32)

        def widen(i):
            peer = chan_peer(i + 1)
            part_all[pl.ds(peer * 16, 16), :] = part_in[peer].astype(f32)

        each(n_chan - 1, widen)
        picks = []
        for k in range(SLOTS):
            row = tab[2 * STATIONS + k // PER] + k % PER
            at = tab[STATIONS + k // PER] * 16 + lax.rem(row, 16)
            picks.append(part_all[at].reshape(1, LANES))
        for k in range(SLOTS, SEL):
            picks.append(jnp.zeros((1, LANES), f32))
        chosen[...] = jnp.concatenate(picks, axis=0).astype(bf16)
        each(n_tm - 1, lambda i: chosen_copy(i).start())

    lane = lax.broadcasted_iota(jnp.int32, (tiles, LANES), 1)

    def prepare(station):
        pieces, squares = [], []
        for d in range(PER):
            move = tab[3 * STATIONS + station * PER + d]
            record = rows[tab[station] + d]
            turned[d] = pltpu.roll(record, lax.rem(LANES - move, LANES), 1)
            here = lane < LANES - move
            parts = [turned[d, pl.ds(b, tiles), :] for b in range(BLOCKS + 1)]
            shifted = [jnp.where(here, parts[b], parts[b + 1]) for b in range(BLOCKS)]
            pieces.append(jnp.concatenate([s.astype(bf16) for s in shifted], axis=1))
            squares.append(jnp.concatenate([(s * s).astype(bf16) for s in shifted], axis=1))
        lhs[station] = jnp.concatenate(pieces, axis=0)
        energy = jnp.dot(jnp.concatenate(squares, axis=0), band[...], preferred_element_type=f32)
        scale[station] = lax.rsqrt(energy / length + EPS) / math.sqrt(length)

    each(STATIONS, prepare)

    for p in range(WAVE_BLOCKS * HALVES):
        @pl.when(now == p)
        def _():
            chosen_all[pl.ds(p * SEL, SEL), :] = chosen[...].astype(f32)

    @pl.when(sends_part)
    def _():
        wait_for(chosen_in, WAVE_BLOCKS * HALVES - 1, sems.at[5])

    @pl.when(jnp.logical_not(sends_part))
    def _():
        wait_for(chosen_in, WAVE_BLOCKS * HALVES, sems.at[5])

    def widen_chosen(i):
        peer = tm_peer(i + 1)

        @pl.when(peer < WAVE_BLOCKS * HALVES)
        def _():
            chosen_all[pl.ds(peer * SEL, SEL), :] = chosen_in[peer].astype(f32)

    each(n_tm - 1, widen_chosen)

    running[0] = jnp.zeros((tiles, LANES), f32)

    def correlate(station, total):
        for d in range(PER):
            k = station * PER + d
            half = (tab[2 * STATIONS + station] + d) // 16
            wave = [chosen_all[(HALVES * b + half) * SEL + k].reshape(1, LANES) for b in range(WAVE_BLOCKS)]
            wave.append(jnp.zeros((1, LANES), f32))
            wide = jnp.broadcast_to(jnp.concatenate(wave, axis=1), (LANES, BLOCKS * LANES))
            toeplitz = pltpu.roll(wide, 0, 1, stride=1, stride_axis=0).astype(bf16)
            numer = lax.dot_general(
                lhs[station, d * tiles : (d + 1) * tiles, :], toeplitz,
                (((1,), (1,)), ((), ())), preferred_element_type=f32,
            )
            total = total + numer * scale[station, d * tiles : (d + 1) * tiles, :]
        running[station + 1] = total
        return total

    lax.fori_loop(0, STATIONS, correlate, jnp.zeros((tiles, LANES), f32))

    ends = 3 * STATIONS + SLOTS

    def summed(template):
        return running[tab[ends + template + 1]] - running[tab[ends + template]]

    def stack_copy(i):
        peer = chan_peer(i + 1)
        return pltpu.make_async_remote_copy(
            src_ref=outgoing.at[peer], dst_ref=incoming.at[me],
            send_sem=sems.at[6], recv_sem=sems.at[7],
            device_id=(peer, now), device_id_type=MESH,
        )

    def send_stack(i):
        peer = chan_peer(i + 1)
        outgoing[peer] = summed(peer).astype(bf16)
        stack_copy(i).start()

    each(n_chan - 1, send_stack)
    stack = summed(me)
    wait_for(incoming, n_chan - 1, sems.at[7])
    stack = lax.fori_loop(
        0, n_chan - 1, lambda i, s: s + incoming[chan_peer(i + 1)].astype(f32), stack
    )
    stack_out[...] = stack
    peak_mine[...] = jnp.broadcast_to(jnp.max(jnp.abs(stack), keepdims=True), peak_mine.shape)

    def peak_copy(i):
        return pltpu.make_async_remote_copy(
            src_ref=peak_mine, dst_ref=peak_in.at[now],
            send_sem=sems.at[8], recv_sem=sems.at[9],
            device_id=(me, tm_peer(i + 1)), device_id_type=MESH,
        )

    each(n_tm - 1, lambda i: peak_copy(i).start())
    wait_for(peak_in, n_tm - 1, sems.at[9])
    peak_out[...] = lax.fori_loop(
        0, n_tm - 1, lambda i, s: jnp.maximum(s, peak_in[tm_peer(i + 1)]), peak_mine[...]
    )

    @pl.when(now > 0)
    def _():
        halo.wait_send()

    @pl.when(sends_part)
    def _():
        wait_for(part_in, n_chan - 1, sems.at[2])
        wait_for(chosen_in, n_tm - 1, sems.at[4])

    wait_for(outgoing, n_chan - 1, sems.at[6])
    wait_for(peak_in, n_tm - 1, sems.at[8])


def tables(channel_list, moveouts, group, channels):
    per_template = channel_list.shape[1] // PER
    first = channel_list[:, ::PER].reshape(-1)
    count = first.shape[0]
    index = jnp.arange(count, dtype=jnp.int32)
    local = first // channels == group
    rank = jnp.sum((index[None, :] < index[:, None]) & local[None, :], axis=1, dtype=jnp.int32)
    hit = ((rank[None, :] == jnp.arange(STATIONS, dtype=jnp.int32)[:, None]) & local[None, :]).astype(jnp.int32)
    chan = jnp.sum(hit * (first - group * channels)[None, :], axis=1)
    template = jnp.sum(hit * (index // per_template)[None, :], axis=1)
    row = jnp.sum(hit * (index % per_template * PER)[None, :], axis=1)
    move = jnp.sum(hit[:, :, None] * moveouts.reshape(1, count, PER), axis=1).reshape(-1)
    edges = jnp.arange(channel_list.shape[0] + 1, dtype=jnp.int32) * per_template
    ends = jnp.sum((index[None, :] < edges[:, None]) & local[None, :], axis=1, dtype=jnp.int32)
    return jnp.concatenate([chan, template, row, move, ends])


def on_device(n_chan, n_tm, seismic, waveforms, channel_list, moveouts):
    channels, piece = seismic.shape
    length = waveforms.shape[2]
    tiles = piece // LANES
    pitch = tiles + 8
    f32, bf16 = jnp.float32, jnp.bfloat16
    tab = tables(channel_list, moveouts, lax.axis_index("chan"), channels)
    stack, peak = pl.pallas_call(
        functools.partial(kernel, n_chan, n_tm, length),
        out_shape=(
            jax.ShapeDtypeStruct((tiles, LANES), f32),
            jax.ShapeDtypeStruct((8, LANES), f32),
        ),
        in_specs=[
            pl.BlockSpec(memory_space=pltpu.SMEM),
            pl.BlockSpec(memory_space=pl.ANY),
            pl.BlockSpec(memory_space=pltpu.VMEM),
        ],
        out_specs=[pl.BlockSpec(memory_space=pltpu.VMEM)] * 2,
        scratch_shapes=[
            pltpu.VMEM((channels, piece), bf16),
            pltpu.VMEM((channels, HALO * LANES), bf16),
            pltpu.VMEM((channels, pitch, LANES), f32),
            pltpu.VMEM((PER, pitch, LANES), f32),
            pltpu.VMEM((STATIONS, PER * tiles, BLOCKS * LANES), bf16),
            pltpu.VMEM((STATIONS, PER * tiles, LANES), f32),
            pltpu.VMEM((BLOCKS * LANES, LANES), bf16),
            pltpu.VMEM((32, WAVE_BLOCKS * LANES), bf16),
            pltpu.VMEM((n_chan, 16, LANES), bf16),
            pltpu.VMEM((n_chan * 16, LANES), f32),
            pltpu.VMEM((SEL, LANES), bf16),
            pltpu.VMEM((n_tm, SEL, LANES), bf16),
            pltpu.VMEM((WAVE_BLOCKS * HALVES * SEL, LANES), f32),
            pltpu.VMEM((STATIONS + 1, tiles, LANES), f32),
            pltpu.VMEM((n_chan, tiles, LANES), bf16),
            pltpu.VMEM((n_chan, tiles, LANES), bf16),
            pltpu.VMEM((8, LANES), f32),
            pltpu.VMEM((n_tm, 8, LANES), f32),
            pltpu.SemaphoreType.DMA((10,)),
            pltpu.SemaphoreType.DMA,
        ],
        compiler_params=pltpu.CompilerParams(
            collective_id=0, has_side_effects=True, vmem_limit_bytes=48 * 1024 * 1024
        ),
    )(tab, seismic, waveforms)
    return stack.reshape(1, piece), peak[0, 0:1]


def solution(mesh):
    return jax.shard_map(
        functools.partial(on_device, mesh.shape["chan"], mesh.shape["tm"]),
        mesh=mesh,
        in_specs=(P("chan", "tm"), P("chan", None, None), P(), P()),
        out_specs=(P("chan", "tm"), P("chan")),
        check_vma=False,
    )
```

```python
import functools
import math

import jax
import jax.numpy as jnp
from jax import lax
from jax.experimental import pallas as pl
from jax.experimental.pallas import tpu as pltpu
from jax.sharding import PartitionSpec as P

LANES = 128
STATIONS = 20
PER = 3
SLOTS = STATIONS * PER
SEL = 64
HALO = 4
BLOCKS = 4
WAVE_BLOCKS = 3
HALVES = 2
PARTS = WAVE_BLOCKS * HALVES
ROW = 4
EPS = 1e-05
MESH = pl.DeviceIdType.MESH


def each(count, body, unroll=1):
    def step(i, carry):
        for u in range(unroll):
            body(i * unroll + u)
        return carry

    assert count % unroll == 0
    lax.fori_loop(0, count // unroll, step, 0)


def before(x, axis):
    index = lax.broadcasted_iota(jnp.int32, x.shape, axis)
    step, total = 1, x
    while step < 32:
        total = total + jnp.where(index >= step, pltpu.roll(total, step, axis), 0)
        step *= 2
    return total - x


def kernel(
    n_chan, n_tm, length, channels,
    listed, moves, seis, waves,
    stack_out, peak_out,
    listed_in, moves_in, waves_in, x_in, halo_in, tab_v, tab,
    rows, turned, lhs, scale, band,
    normed, part_in, part_all, chosen, chosen_in, chosen_all,
    running, outgoing, incoming, peak_mine, peak_in,
    sems, in_sems,
):
    me = lax.axis_index("chan")
    now = lax.axis_index("tm")
    core = lax.rem(me, HALVES)
    across = lax.rem(now, ROW)
    row_start = now - across
    sibling = me + 1 - 2 * core
    tiles = stack_out.shape[0]
    pitch = rows.shape[1]
    flat_rows = rows.reshape(channels * pitch, LANES)
    half_tiles = tiles // 2
    f32, bf16, i32 = jnp.float32, jnp.bfloat16, jnp.int32

    def wait_for(ref, blocks, sem):
        span = ref.at[pl.ds(0, blocks)]
        pltpu.make_async_copy(span, span, sem).wait()

    def chan_peer(d):
        return lax.rem(me + d, n_chan)

    def tm_peer(d):
        return lax.rem(now + d, n_tm)

    def row_peer(d):
        return row_start + lax.rem(across + d, ROW)

    barrier = pltpu.get_barrier_semaphore()

    def greet(group, piece):
        pl.semaphore_signal(barrier, inc=1, device_id=(group, piece), device_id_type=MESH)

    each(n_chan - 1, lambda i: greet(chan_peer(i + 1), now))
    each(n_tm - 1, lambda i: greet(me, tm_peer(i + 1)))
    each(ROW - 1, lambda i: greet(sibling, row_peer(i + 1)))

    loads = [
        pltpu.make_async_copy(src, dst, in_sems.at[i])
        for i, (src, dst) in enumerate(
            ((waves, waves_in), (listed, listed_in), (moves, moves_in), (seis, x_in))
        )
    ]
    for copy in loads:
        copy.start()

    lag = lax.broadcasted_iota(i32, band.shape, 0) - lax.broadcasted_iota(i32, band.shape, 1)
    band[...] = jnp.where((lag >= 0) & (lag < length), 1.0, 0.0).astype(bf16)

    loads[0].wait()
    w = waves_in[0]
    centered = w - jnp.mean(w, axis=-1, keepdims=True)
    factor = lax.rsqrt(jnp.mean(centered * centered, axis=-1, keepdims=True) + EPS) / math.sqrt(length)
    normed[...] = jnp.zeros_like(normed)
    normed[0 : w.shape[0], 0:length] = (centered * factor).astype(bf16)

    pl.semaphore_wait(barrier, n_chan - 1 + n_tm - 1 + ROW - 1)

    halo = pltpu.make_async_remote_copy(
        src_ref=seis.at[:, pl.ds(0, HALO * LANES)], dst_ref=halo_in,
        send_sem=sems.at[0], recv_sem=sems.at[1],
        device_id=(me, jnp.maximum(now - 1, 0)), device_id_type=MESH,
    )

    sends_part = across < WAVE_BLOCKS
    block_of = jnp.minimum(across, WAVE_BLOCKS - 1)

    def part(half):
        return normed.at[pl.ds(half * 16, 16), pl.ds(block_of * LANES, LANES)]

    def part_copy(i):
        peer = chan_peer(i + 1)
        return pltpu.make_async_remote_copy(
            src_ref=part(lax.rem(peer, HALVES)), dst_ref=part_in.at[me],
            send_sem=sems.at[2], recv_sem=sems.at[3],
            device_id=(peer, now), device_id_type=MESH,
        )

    @pl.when(sends_part)
    def _():
        each(n_chan - 1, lambda i: part_copy(i).start())

    @pl.when(now > 0)
    def _():
        halo.start()

    loads[1].wait()
    loads[2].wait()
    templates, per_template = listed_in.shape
    names = listed_in[...]
    column = lax.broadcasted_iota(i32, names.shape, 1)
    key = jnp.full(names.shape, -1, i32)
    code = (lax.broadcasted_iota(i32, names.shape, 0) * 32 + column) * LANES + moves_in[...]
    counts = jnp.zeros((templates, 1), i32)
    for place, group in ((0, me), (SEL, sibling)):
        from_first = names - group * channels
        inside = (from_first >= 0) & (from_first < channels)
        mine = jnp.where(inside, 1, 0)
        in_row = before(mine, 1)
        full_row = jnp.sum(mine, axis=1, keepdims=True)
        rank = in_row + before(jnp.broadcast_to(full_row, mine.shape), 0)
        key = jnp.where(inside & (rank < SLOTS), rank + place, key)
        code = jnp.where(inside, code + from_first * (1 << 17), code)
        if place == 0:
            counts = full_row
    lane32 = lax.broadcasted_iota(i32, (templates, LANES), 1)
    found = jnp.zeros((templates, LANES), i32)
    for c in range(per_template):
        found = found + jnp.where(
            lane32 == jnp.broadcast_to(key[:, c : c + 1], lane32.shape),
            jnp.broadcast_to(code[:, c : c + 1], lane32.shape), 0,
        )
    ahead = jnp.where(
        lax.broadcasted_iota(i32, lane32.shape, 0) < lane32, jnp.broadcast_to(counts, lane32.shape), 0
    )
    tab_v[0:1, :] = jnp.sum(found, axis=0, keepdims=True)
    tab_v[1:2, :] = jnp.minimum(jnp.sum(ahead, axis=0, keepdims=True), SLOTS)
    to_scalars = pltpu.make_async_copy(tab_v, tab, in_sems.at[4])
    to_scalars.start()

    def lay(ref, first):
        for i in range(ref.shape[1] // LANES):
            for c in range(0, channels, 16):
                flat_rows[pl.ds(c * pitch + first + i, 16, stride=pitch), :] = ref[
                    c : c + 16, i * LANES : (i + 1) * LANES
                ].astype(f32)

    loads[3].wait()
    lay(x_in, 0)
    to_scalars.wait()

    def template_of(code):
        return (code >> 12) & 31

    def row_of(code):
        return (code >> 7) & 31

    lane = lax.broadcasted_iota(i32, (half_tiles, LANES), 1)
    together = 4

    def prepare(group, half):
        squares = []
        first = half * half_tiles
        for u in range(together):
            station = group * together + u
            for d in range(PER):
                entry = tab[0, station * PER + d]
                move = entry & (LANES - 1)
                record = rows[entry >> 17][first : first + half_tiles + 8]
                at = u * PER + d
                turned[at] = pltpu.roll(record, lax.rem(LANES - move, LANES), 1)
                here = lane < LANES - move
                parts = [turned[at, b : b + half_tiles, :] for b in range(BLOCKS + 1)]
                shifted = [jnp.where(here, parts[b], parts[b + 1]) for b in range(BLOCKS)]
                lhs[station, d, first : first + half_tiles, :] = jnp.concatenate(
                    [s.astype(bf16) for s in shifted], axis=1
                )
                squares.append(jnp.concatenate([(s * s).astype(bf16) for s in shifted], axis=1))
        energy = jnp.dot(jnp.concatenate(squares, axis=0), band[...], preferred_element_type=f32)
        factor = lax.rsqrt(energy / length + EPS) / math.sqrt(length)
        for u in range(together):
            for d in range(PER):
                at = (u * PER + d) * half_tiles
                scale[group * together + u, d, first : first + half_tiles, :] = factor[at : at + half_tiles]

    each(STATIONS // together, lambda g: prepare(g, 0))

    def chosen_copy(other, d):
        return pltpu.make_async_remote_copy(
            src_ref=chosen.at[other], dst_ref=chosen_in.at[block_of * HALVES + core],
            send_sem=sems.at[4], recv_sem=sems.at[5],
            device_id=(sibling if other else me, row_peer(d)), device_id_type=MESH,
        )

    @pl.when(sends_part)
    def _():
        wait_for(part_in, n_chan - 1, sems.at[3])
        part_all[pl.ds(me * 16, 16), :] = part(core)[...].astype(f32)

        def widen(i):
            peer = chan_peer(i + 1)
            part_all[pl.ds(peer * 16, 16), :] = part_in[peer].astype(f32)

        for i in range(n_chan - 1):
            widen(i)
        for other in (1, 0):
            picks = []
            for k in range(SLOTS):
                entry = tab[0, other * SEL + k]
                at = template_of(entry) * 16 + (row_of(entry) & 15)
                picks.append(part_all[at].reshape(1, LANES))
            for k in range(SLOTS, SEL):
                picks.append(jnp.zeros((1, LANES), f32))
            chosen[other] = jnp.concatenate(picks, axis=0).astype(bf16)
            if other:
                chosen_copy(1, 0).start()
            for d in (2, 1, 3):
                chosen_copy(other, d).start()

    @pl.when(now < n_tm - 1)
    def _():
        halo.wait_recv()

    @pl.when(now == n_tm - 1)
    def _():
        halo_in[...] = jnp.zeros_like(halo_in)

    lay(halo_in, tiles)
    each(STATIONS // together, lambda g: prepare(g, 1))

    @pl.when(sends_part)
    def _():
        wait_for(chosen_in, PARTS - 1, sems.at[5])

    @pl.when(jnp.logical_not(sends_part))
    def _():
        wait_for(chosen_in, PARTS, sems.at[5])

    for p in range(PARTS):
        own = sends_part & (block_of * HALVES + core == p)

        @pl.when(own)
        def _():
            chosen_all[p * SEL : (p + 1) * SEL, :] = chosen[0].astype(f32)

        @pl.when(jnp.logical_not(own))
        def _():
            chosen_all[p * SEL : (p + 1) * SEL, :] = chosen_in[p].astype(f32)

    running[0] = jnp.zeros((tiles, LANES), f32)

    def correlate(group, total):
        for u in range(together):
            station = group * together + u
            for d in range(PER):
                k = station * PER + d
                half = row_of(tab[0, k]) >> 4
                wave = [chosen_all[(HALVES * b + half) * SEL + k].reshape(1, LANES) for b in range(WAVE_BLOCKS)]
                wave.append(jnp.zeros((1, LANES), f32))
                wide = jnp.broadcast_to(jnp.concatenate(wave, axis=1), (LANES, BLOCKS * LANES))
                toeplitz = pltpu.roll(wide, 0, 1, stride=1, stride_axis=0).astype(bf16)
                numer = lax.dot_general(
                    lhs[station, d], toeplitz, (((1,), (1,)), ((), ())), preferred_element_type=f32,
                )
                total = total + numer * scale[station, d]
            running[station + 1] = total
        return total

    lax.fori_loop(0, STATIONS // together, correlate, jnp.zeros((tiles, LANES), f32))

    def summed(template):
        return running[tab[1, template + 1] // PER] - running[tab[1, template] // PER]

    def stack_copy(i):
        peer = chan_peer(i + 1)
        return pltpu.make_async_remote_copy(
            src_ref=outgoing.at[peer], dst_ref=incoming.at[me],
            send_sem=sems.at[6], recv_sem=sems.at[7],
            device_id=(peer, now), device_id_type=MESH,
        )

    def send_stack(i):
        peer = chan_peer(i + 1)
        outgoing[peer] = summed(peer).astype(bf16)
        stack_copy(i).start()

    for i in range(n_chan - 1):
        send_stack(i)
    stack = summed(me)
    wait_for(incoming, n_chan - 1, sems.at[7])
    for i in range(n_chan - 1):
        stack = stack + incoming[chan_peer(i + 1)].astype(f32)
    stack_out[...] = stack
    peak_mine[...] = jnp.broadcast_to(jnp.max(jnp.abs(stack), keepdims=True), peak_mine.shape)

    def peak_copy(i):
        return pltpu.make_async_remote_copy(
            src_ref=peak_mine, dst_ref=peak_in.at[now],
            send_sem=sems.at[8], recv_sem=sems.at[9],
            device_id=(me, tm_peer(i + 1)), device_id_type=MESH,
        )

    for i in range(n_tm - 1):
        peak_copy(i).start()
    wait_for(peak_in, n_tm - 1, sems.at[9])
    peak = peak_mine[...]
    for i in range(n_tm - 1):
        peak = jnp.maximum(peak, peak_in[tm_peer(i + 1)])
    peak_out[...] = peak

    @pl.when(now > 0)
    def _():
        halo.wait_send()

    @pl.when(sends_part)
    def _():
        wait_for(part_in, n_chan - 1, sems.at[2])
        wait_for(chosen_in, 2 * ROW - 1, sems.at[4])

    wait_for(outgoing, n_chan - 1, sems.at[6])
    wait_for(peak_in, n_tm - 1, sems.at[8])


def on_device(n_chan, n_tm, seismic, waveforms, channel_list, moveouts):
    channels, piece = seismic.shape
    length = waveforms.shape[2]
    tiles = piece // LANES
    pitch = tiles + 8
    f32, bf16, i32 = jnp.float32, jnp.bfloat16, jnp.int32
    stack, peak = pl.pallas_call(
        functools.partial(kernel, n_chan, n_tm, length, channels),
        out_shape=(
            jax.ShapeDtypeStruct((tiles, LANES), f32),
            jax.ShapeDtypeStruct((8, LANES), f32),
        ),
        in_specs=[pl.BlockSpec(memory_space=pltpu.HBM)] * 4,
        out_specs=[pl.BlockSpec(memory_space=pltpu.VMEM)] * 2,
        scratch_shapes=[
            pltpu.VMEM(channel_list.shape, i32),
            pltpu.VMEM(moveouts.shape, i32),
            pltpu.VMEM(waveforms.shape, f32),
            pltpu.VMEM((channels, piece), bf16),
            pltpu.VMEM((channels, HALO * LANES), bf16),
            pltpu.VMEM((8, LANES), i32),
            pltpu.SMEM((8, LANES), i32),
            pltpu.VMEM((channels, pitch, LANES), f32),
            pltpu.VMEM((4 * PER, tiles // 2 + 8, LANES), f32),
            pltpu.VMEM((STATIONS, PER, tiles, BLOCKS * LANES), bf16),
            pltpu.VMEM((STATIONS, PER, tiles, LANES), f32),
            pltpu.VMEM((BLOCKS * LANES, LANES), bf16),
            pltpu.VMEM((32, WAVE_BLOCKS * LANES), bf16),
            pltpu.VMEM((n_chan, 16, LANES), bf16),
            pltpu.VMEM((n_chan * 16, LANES), f32),
            pltpu.VMEM((2, SEL, LANES), bf16),
            pltpu.VMEM((2 * ROW, SEL, LANES), bf16),
            pltpu.VMEM((PARTS * SEL, LANES), f32),
            pltpu.VMEM((STATIONS + 1, tiles, LANES), f32),
            pltpu.VMEM((n_chan, tiles, LANES), bf16),
            pltpu.VMEM((n_chan, tiles, LANES), bf16),
            pltpu.VMEM((8, LANES), f32),
            pltpu.VMEM((n_tm, 8, LANES), f32),
            pltpu.SemaphoreType.DMA((10,)),
            pltpu.SemaphoreType.DMA((5,)),
        ],
        compiler_params=pltpu.CompilerParams(
            collective_id=0, has_side_effects=True, vmem_limit_bytes=48 * 1024 * 1024
        ),
    )(channel_list, moveouts, seismic, waveforms)
    return stack.reshape(1, piece), peak[0, 0:1]


def solution(mesh):
    return jax.shard_map(
        functools.partial(on_device, mesh.shape["chan"], mesh.shape["tm"]),
        mesh=mesh,
        in_specs=(P("chan", "tm"), P("chan", None, None), P(), P()),
        out_specs=(P("chan", "tm"), P("chan")),
        check_vma=False,
    )
```

```python
import functools
import math

import jax
import jax.numpy as jnp
from jax import lax
from jax.experimental import pallas as pl
from jax.experimental.pallas import tpu as pltpu
from jax.sharding import PartitionSpec as P

LANES = 128
STATIONS = 20
PER = 3
SLOTS = STATIONS * PER
SEL = 64
HALO = 4
BLOCKS = 4
WAVE_BLOCKS = 3
HALVES = 2
PARTS = WAVE_BLOCKS * HALVES
ROW = 4
RING = 8
EPS = 1e-05
GRANT = 55200 * 1024
MESH = pl.DeviceIdType.MESH


def each(count, body, unroll=1):
    def step(i, carry):
        for u in range(unroll):
            body(i * unroll + u)
        return carry

    assert count % unroll == 0
    lax.fori_loop(0, count // unroll, step, 0)


def ring_offsets(n_chan):
    chips = n_chan // HALVES
    depth = min(RING, chips)
    offsets = [(dy, dz) for dy in range(chips // depth) for dz in range(depth)]
    return sorted(offsets, key=lambda o: (-(o[0] + min(o[1], depth - o[1])), o))


def before(x, axis):
    index = lax.broadcasted_iota(jnp.int32, x.shape, axis)
    step, total = 1, x
    while step < 32:
        total = total + jnp.where(index >= step, pltpu.roll(total, step, axis), 0)
        step *= 2
    return total - x


def kernel(
    n_chan, n_tm, length, channels,
    listed, moves, seis, waves,
    stack_out, peak_out,
    listed_in, moves_in, waves_in, x_in, halo_in, tab_v, tab,
    rows, turned, lhs, scale, band,
    normed, part_in, part_all, chosen, chosen_in, chosen_all,
    running, pair_out, pair_in, outgoing, incoming, peak_mine, peak_in,
    sems, in_sems,
):
    me = lax.axis_index("chan")
    now = lax.axis_index("tm")
    core = lax.rem(me, HALVES)
    across = lax.rem(now, ROW)
    row_start = now - across
    sibling = me + 1 - 2 * core
    tiles = stack_out.shape[0]
    pitch = rows.shape[1]
    flat_rows = rows.reshape(channels * pitch, LANES)
    half_tiles = tiles // 2
    f32, bf16, i32 = jnp.float32, jnp.bfloat16, jnp.int32

    def wait_for(ref, blocks, sem):
        span = ref.at[pl.ds(0, blocks)]
        pltpu.make_async_copy(span, span, sem).wait()

    chip = me // HALVES
    depth = min(RING, n_chan // HALVES)
    offsets = ring_offsets(n_chan)

    def chip_at(offset):
        dy, dz = offset
        y, z = chip // depth, lax.rem(chip, depth)
        return lax.rem(y + dy, n_chan // HALVES // depth) * depth + lax.rem(z + dz, depth)

    chan_peers = [
        chip_at(offset) * HALVES + lax.rem(core + dc, HALVES)
        for offset in offsets for dc in range(HALVES) if offset != (0, 0) or dc
    ]
    far_chips = [chip_at(offset) for offset in offsets if offset != (0, 0)]

    def tm_peer(d):
        return lax.rem(now + d, n_tm)

    def row_peer(d):
        return row_start + lax.rem(across + d, ROW)

    barrier = pltpu.get_barrier_semaphore()

    def greet(group, piece):
        pl.semaphore_signal(barrier, inc=1, device_id=(group, piece), device_id_type=MESH)

    for peer in chan_peers[: n_chan // 2]:
        greet(peer, now)
    for i in range(n_tm - 1):
        greet(me, tm_peer(i + 1))
    for i in range(ROW - 1):
        greet(sibling, row_peer(i + 1))
    for peer in chan_peers[n_chan // 2 :]:
        greet(peer, now)

    loads = [
        pltpu.make_async_copy(src, dst, in_sems.at[i])
        for i, (src, dst) in enumerate(
            ((waves, waves_in), (listed, listed_in), (moves, moves_in), (seis, x_in))
        )
    ]
    for copy in loads:
        copy.start()

    lag = lax.broadcasted_iota(i32, band.shape, 0) - lax.broadcasted_iota(i32, band.shape, 1)
    band[...] = jnp.where((lag >= 0) & (lag < length), 1.0, 0.0).astype(bf16)

    loads[0].wait()
    w = waves_in[:, 0, :]
    centered = w - jnp.mean(w, axis=-1, keepdims=True)
    factor = lax.rsqrt(jnp.mean(centered * centered, axis=-1, keepdims=True) + EPS) / math.sqrt(length)
    normed[...] = jnp.zeros_like(normed)
    normed[0 : w.shape[0], 0:length] = (centered * factor).astype(bf16)

    pl.semaphore_wait(barrier, n_chan - 1 + n_tm - 1 + ROW - 1)

    halo = pltpu.make_async_remote_copy(
        src_ref=seis.at[:, pl.ds(0, HALO * LANES)], dst_ref=halo_in,
        send_sem=sems.at[0], recv_sem=sems.at[1],
        device_id=(me, jnp.maximum(now - 1, 0)), device_id_type=MESH,
    )

    sends_part = across < WAVE_BLOCKS
    block_of = jnp.minimum(across, WAVE_BLOCKS - 1)

    def part(half):
        return normed.at[pl.ds(half * 16, 16), pl.ds(block_of * LANES, LANES)]

    def part_copy(peer):
        return pltpu.make_async_remote_copy(
            src_ref=part(lax.rem(peer, HALVES)), dst_ref=part_in.at[me],
            send_sem=sems.at[2], recv_sem=sems.at[3],
            device_id=(peer, now), device_id_type=MESH,
        )

    @pl.when(sends_part)
    def _():
        for peer in chan_peers:
            part_copy(peer).start()

    @pl.when(now > 0)
    def _():
        halo.start()

    loads[1].wait()
    loads[2].wait()
    templates, per_template = listed_in.shape
    names = listed_in[...]
    column = lax.broadcasted_iota(i32, names.shape, 1)
    key = jnp.full(names.shape, -1, i32)
    code = (lax.broadcasted_iota(i32, names.shape, 0) * 32 + column) * LANES + moves_in[...]
    counts = jnp.zeros((templates, 1), i32)
    for place, group in ((0, me), (SEL, sibling)):
        from_first = names - group * channels
        inside = (from_first >= 0) & (from_first < channels)
        mine = jnp.where(inside, 1, 0)
        in_row = before(mine, 1)
        full_row = jnp.sum(mine, axis=1, keepdims=True)
        rank = in_row + before(jnp.broadcast_to(full_row, mine.shape), 0)
        key = jnp.where(inside & (rank < SLOTS), rank + place, key)
        code = jnp.where(inside, code + from_first * (1 << 17), code)
        if place == 0:
            counts = full_row
    lane32 = lax.broadcasted_iota(i32, (templates, LANES), 1)
    found = jnp.zeros((templates, LANES), i32)
    for c in range(per_template):
        found = found + jnp.where(
            lane32 == jnp.broadcast_to(key[:, c : c + 1], lane32.shape),
            jnp.broadcast_to(code[:, c : c + 1], lane32.shape), 0,
        )
    ahead = jnp.where(
        lax.broadcasted_iota(i32, lane32.shape, 0) < lane32, jnp.broadcast_to(counts, lane32.shape), 0
    )
    tab_v[0:1, :] = jnp.sum(found, axis=0, keepdims=True)
    tab_v[1:2, :] = jnp.minimum(jnp.sum(ahead, axis=0, keepdims=True), SLOTS)
    to_scalars = pltpu.make_async_copy(tab_v, tab, in_sems.at[4])
    to_scalars.start()

    def lay(ref, first):
        for i in range(ref.shape[1] // LANES):
            for c in range(0, channels, 16):
                flat_rows[pl.ds(c * pitch + first + i, 16, stride=pitch), :] = ref[
                    c : c + 16, i * LANES : (i + 1) * LANES
                ].astype(f32)

    loads[3].wait()
    lay(x_in, 0)
    to_scalars.wait()

    def template_of(code):
        return (code >> 12) & 31

    def row_of(code):
        return (code >> 7) & 31

    lane = lax.broadcasted_iota(i32, (half_tiles, LANES), 1)
    together = 4

    def prepare(group, half):
        squares = []
        first = half * half_tiles
        for u in range(together):
            station = group * together + u
            for d in range(PER):
                entry = tab[0, station * PER + d]
                move = entry & (LANES - 1)
                record = rows[entry >> 17][first : first + half_tiles + 8]
                at = u * PER + d
                turned[at] = pltpu.roll(record, lax.rem(LANES - move, LANES), 1)
                here = lane < LANES - move
                parts = [turned[at, b : b + half_tiles, :] for b in range(BLOCKS + 1)]
                shifted = [jnp.where(here, parts[b], parts[b + 1]) for b in range(BLOCKS)]
                lhs[station, d, first : first + half_tiles, :] = jnp.concatenate(
                    [s.astype(bf16) for s in shifted], axis=1
                )
                squares.append(jnp.concatenate([(s * s).astype(bf16) for s in shifted], axis=1))
        energy = jnp.dot(jnp.concatenate(squares, axis=0), band[...], preferred_element_type=f32)
        factor = lax.rsqrt(energy / length + EPS) / math.sqrt(length)
        for u in range(together):
            for d in range(PER):
                at = (u * PER + d) * half_tiles
                scale[group * together + u, d, first : first + half_tiles, :] = factor[at : at + half_tiles]

    each(STATIONS // together, lambda g: prepare(g, 0))

    def chosen_copy(other, d):
        return pltpu.make_async_remote_copy(
            src_ref=chosen.at[other], dst_ref=chosen_in.at[block_of * HALVES + core],
            send_sem=sems.at[4], recv_sem=sems.at[5],
            device_id=(sibling if other else me, row_peer(d)), device_id_type=MESH,
        )

    @pl.when(sends_part)
    def _():
        wait_for(part_in, n_chan - 1, sems.at[3])
        part_all[pl.ds(me * 16, 16), :] = part(core)[...].astype(f32)

        for peer in chan_peers:
            part_all[pl.ds(peer * 16, 16), :] = part_in[peer].astype(f32)
        for other in (1, 0):
            picks = []
            for k in range(SLOTS):
                entry = tab[0, other * SEL + k]
                at = template_of(entry) * 16 + (row_of(entry) & 15)
                picks.append(part_all[at].reshape(1, LANES))
            for k in range(SLOTS, SEL):
                picks.append(jnp.zeros((1, LANES), f32))
            chosen[other] = jnp.concatenate(picks, axis=0).astype(bf16)
            if other:
                chosen_copy(1, 0).start()
            for d in (2, 1, 3):
                chosen_copy(other, d).start()

    @pl.when(now < n_tm - 1)
    def _():
        halo.wait_recv()

    @pl.when(now == n_tm - 1)
    def _():
        halo_in[...] = jnp.zeros_like(halo_in)

    lay(halo_in, tiles)
    each(STATIONS // together, lambda g: prepare(g, 1))

    @pl.when(sends_part)
    def _():
        wait_for(chosen_in, PARTS - 1, sems.at[5])

    @pl.when(jnp.logical_not(sends_part))
    def _():
        wait_for(chosen_in, PARTS, sems.at[5])

    for p in range(PARTS):
        own = sends_part & (block_of * HALVES + core == p)

        @pl.when(own)
        def _():
            chosen_all[p * SEL : (p + 1) * SEL, :] = chosen[0].astype(f32)

        @pl.when(jnp.logical_not(own))
        def _():
            chosen_all[p * SEL : (p + 1) * SEL, :] = chosen_in[p].astype(f32)

    running[0] = jnp.zeros((tiles, LANES), f32)

    at_once = 10

    def correlate(group, total):
        for u in range(at_once):
            station = group * at_once + u
            for d in range(PER):
                k = station * PER + d
                half = row_of(tab[0, k]) >> 4
                wave = [chosen_all[(HALVES * b + half) * SEL + k].reshape(1, LANES) for b in range(WAVE_BLOCKS)]
                wave.append(jnp.zeros((1, LANES), f32))
                wide = jnp.broadcast_to(jnp.concatenate(wave, axis=1), (LANES, BLOCKS * LANES))
                toeplitz = pltpu.roll(wide, 0, 1, stride=1, stride_axis=0).astype(bf16)
                numer = lax.dot_general(
                    lhs[station, d], toeplitz, (((1,), (1,)), ((), ())), preferred_element_type=f32,
                )
                total = total + numer * scale[station, d]
            running[station + 1] = total
        return total

    lax.fori_loop(0, STATIONS // at_once, correlate, jnp.zeros((tiles, LANES), f32))

    def summed(template):
        return running[tab[1, template + 1] // PER] - running[tab[1, template] // PER]

    pair = pltpu.make_async_remote_copy(
        src_ref=pair_out, dst_ref=pair_in, send_sem=sems.at[10], recv_sem=sems.at[11],
        device_id=(sibling, now), device_id_type=MESH,
    )
    for i in range(n_chan // HALVES):
        pair_out[i] = summed(i * HALVES + 1 - core)
    pair.start()

    def stack_copy(place):
        return pltpu.make_async_remote_copy(
            src_ref=outgoing.at[place], dst_ref=incoming.at[chip],
            send_sem=sems.at[6], recv_sem=sems.at[7],
            device_id=(place * HALVES + core, now), device_id_type=MESH,
        )

    pair.wait_recv()
    for place in far_chips:
        outgoing[place] = (summed(place * HALVES + core) + pair_in[place]).astype(bf16)
        stack_copy(place).start()
    stack = summed(me) + pair_in[chip]
    if far_chips:
        wait_for(incoming, len(far_chips), sems.at[7])
    for place in far_chips:
        stack = stack + incoming[place].astype(f32)
    stack_out[...] = stack
    peak_mine[...] = jnp.max(jnp.abs(stack).reshape(tiles // 8, 8, LANES), axis=0)

    def peak_copy(i):
        return pltpu.make_async_remote_copy(
            src_ref=peak_mine, dst_ref=peak_in.at[now],
            send_sem=sems.at[8], recv_sem=sems.at[9],
            device_id=(me, tm_peer(i + 1)), device_id_type=MESH,
        )

    for i in range(n_tm - 1):
        peak_copy(i).start()
    wait_for(peak_in, n_tm - 1, sems.at[9])
    peak = peak_mine[...]
    for i in range(n_tm - 1):
        peak = jnp.maximum(peak, peak_in[tm_peer(i + 1)])
    peak_out[...] = peak

    @pl.when(now > 0)
    def _():
        halo.wait_send()

    @pl.when(sends_part)
    def _():
        wait_for(part_in, n_chan - 1, sems.at[2])
        wait_for(chosen_in, 2 * ROW - 1, sems.at[4])

    pair.wait_send()
    if far_chips:
        wait_for(outgoing, len(far_chips), sems.at[6])
    wait_for(peak_in, n_tm - 1, sems.at[8])


def on_device(n_chan, n_tm, seismic, waveforms, channel_list, moveouts):
    channels, piece = seismic.shape
    length = waveforms.shape[2]
    tiles = piece // LANES
    pitch = tiles + 8
    f32, bf16, i32 = jnp.float32, jnp.bfloat16, jnp.int32
    stack, peak = pl.pallas_call(
        functools.partial(kernel, n_chan, n_tm, length, channels),
        out_shape=(
            jax.ShapeDtypeStruct((tiles, LANES), f32),
            jax.ShapeDtypeStruct((8, LANES), f32),
        ),
        in_specs=[pl.BlockSpec(memory_space=pltpu.HBM)] * 4,
        out_specs=[pl.BlockSpec(memory_space=pltpu.VMEM)] * 2,
        scratch_shapes=[
            pltpu.VMEM(channel_list.shape, i32),
            pltpu.VMEM(moveouts.shape, i32),
            pltpu.VMEM((waveforms.shape[1], 1, length), f32),
            pltpu.VMEM((channels, piece), bf16),
            pltpu.VMEM((channels, HALO * LANES), bf16),
            pltpu.VMEM((8, LANES), i32),
            pltpu.SMEM((8, LANES), i32),
            pltpu.VMEM((channels, pitch, LANES), f32),
            pltpu.VMEM((4 * PER, tiles // 2 + 8, LANES), f32),
            pltpu.VMEM((STATIONS, PER, tiles, BLOCKS * LANES), bf16),
            pltpu.VMEM((STATIONS, PER, tiles, LANES), f32),
            pltpu.VMEM((BLOCKS * LANES, LANES), bf16),
            pltpu.VMEM((32, WAVE_BLOCKS * LANES), bf16),
            pltpu.VMEM((n_chan, 16, LANES), bf16),
            pltpu.VMEM((n_chan * 16, LANES), f32),
            pltpu.VMEM((2, SEL, LANES), bf16),
            pltpu.VMEM((2 * ROW, SEL, LANES), bf16),
            pltpu.VMEM((PARTS * SEL, LANES), f32),
            pltpu.VMEM((STATIONS + 1, tiles, LANES), f32),
            pltpu.VMEM((n_chan // HALVES, tiles, LANES), f32),
            pltpu.VMEM((n_chan // HALVES, tiles, LANES), f32),
            pltpu.VMEM((n_chan // HALVES, tiles, LANES), bf16),
            pltpu.VMEM((n_chan // HALVES, tiles, LANES), bf16),
            pltpu.VMEM((8, LANES), f32),
            pltpu.VMEM((n_tm, 8, LANES), f32),
            pltpu.SemaphoreType.DMA((12,)),
            pltpu.SemaphoreType.DMA((5,)),
        ],
        compiler_params=pltpu.CompilerParams(
            collective_id=0, has_side_effects=True, vmem_limit_bytes=GRANT
        ),
    )(channel_list, moveouts, seismic, jnp.transpose(waveforms, (1, 0, 2)))
    return stack.reshape(1, piece), jnp.max(peak).reshape(1)


def solution(mesh):
    return jax.shard_map(
        functools.partial(on_device, mesh.shape["chan"], mesh.shape["tm"]),
        mesh=mesh,
        in_specs=(P("chan", "tm"), P("chan", None, None), P(), P()),
        out_specs=(P("chan", "tm"), P("chan")),
        check_vma=False,
    )
```

```python
import functools
import math

import jax
import jax.numpy as jnp
from jax import lax
from jax.experimental import pallas as pl
from jax.experimental.pallas import tpu as pltpu
from jax.sharding import PartitionSpec as P

LANES = 128
HALF_LANES = 64
STATIONS = 20
PER = 3
SLOTS = STATIONS * PER
SEL = 64
HALO = 4
BLOCKS = 4
WAVE_BLOCKS = 3
HALVES = 2
PARTS = WAVE_BLOCKS * HALVES
ROW = 4
RING = 8
EPS = 1e-05
GRANT = 55200 * 1024
MESH = pl.DeviceIdType.MESH


def each(count, body, unroll=1):
    def step(i, carry):
        for u in range(unroll):
            body(i * unroll + u)
        return carry

    assert count % unroll == 0
    lax.fori_loop(0, count // unroll, step, 0)


def ring_offsets(n_chan):
    chips = n_chan // HALVES
    depth = min(RING, chips)
    offsets = [(dy, dz) for dy in range(chips // depth) for dz in range(depth)]
    return sorted(offsets, key=lambda o: (-(o[0] + min(o[1], depth - o[1])), o))


def before(x, axis):
    index = lax.broadcasted_iota(jnp.int32, x.shape, axis)
    step, total = 1, x
    while step < 32:
        total = total + jnp.where(index >= step, pltpu.roll(total, step, axis), 0)
        step *= 2
    return total - x


def kernel(
    n_chan, n_tm, length, channels,
    listed, moves, seis, waves,
    stack_out, peak_out,
    listed_in, moves_in, waves_in, x_in, halo_in, tab_v, tab,
    rows, turned, lhs, scale, band,
    normed, part_in, part_all, chosen, chosen_in, chosen_all,
    running, pair_out, pair_in, outgoing, incoming, peak_mine, peak_in,
    sems, in_sems,
):
    me = lax.axis_index("chan")
    now = lax.axis_index("tm")
    core = lax.rem(me, HALVES)
    across = lax.rem(now, ROW)
    row_start = now - across
    sibling = me + 1 - 2 * core
    tiles = stack_out.shape[0]
    pitch = rows.shape[1]
    flat_rows = rows.reshape(channels * pitch, LANES)
    half_tiles = tiles // 2
    f32, bf16, i32 = jnp.float32, jnp.bfloat16, jnp.int32

    def wait_for(ref, blocks, sem):
        span = ref.at[pl.ds(0, blocks)]
        pltpu.make_async_copy(span, span, sem).wait()

    chip = me // HALVES
    depth = min(RING, n_chan // HALVES)
    offsets = ring_offsets(n_chan)

    def chip_at(offset):
        dy, dz = offset
        y, z = chip // depth, lax.rem(chip, depth)
        return lax.rem(y + dy, n_chan // HALVES // depth) * depth + lax.rem(z + dz, depth)

    chan_peers = [
        chip_at(offset) * HALVES + lax.rem(core + dc, HALVES)
        for offset in offsets for dc in range(HALVES) if offset != (0, 0) or dc
    ]
    far_chips = [chip_at(offset) for offset in offsets if offset != (0, 0)]

    def tm_peer(d):
        return lax.rem(now + d, n_tm)

    def row_peer(d):
        return row_start + lax.rem(across + d, ROW)

    barrier = pltpu.get_barrier_semaphore()

    def greet(group, piece):
        pl.semaphore_signal(barrier, inc=1, device_id=(group, piece), device_id_type=MESH)

    for peer in chan_peers[: n_chan // 2]:
        greet(peer, now)
    for i in range(n_tm - 1):
        greet(me, tm_peer(i + 1))
    for i in range(ROW - 1):
        greet(sibling, row_peer(i + 1))
    for peer in chan_peers[n_chan // 2 :]:
        greet(peer, now)

    loads = [
        pltpu.make_async_copy(src, dst, in_sems.at[i])
        for i, (src, dst) in enumerate(
            ((waves, waves_in), (listed, listed_in), (moves, moves_in), (seis, x_in))
        )
    ]
    for copy in loads:
        copy.start()

    lag = lax.broadcasted_iota(i32, band.shape, 0) - lax.broadcasted_iota(i32, band.shape, 1)
    band[...] = jnp.where((lag >= 0) & (lag < length), 1.0, 0.0).astype(bf16)

    loads[0].wait()
    w = waves_in[:, 0, :]
    centered = w - jnp.mean(w, axis=-1, keepdims=True)
    factor = lax.rsqrt(jnp.mean(centered * centered, axis=-1, keepdims=True) + EPS) / math.sqrt(length)
    normed[...] = jnp.zeros_like(normed)
    normed[0 : w.shape[0], 0:length] = (centered * factor).astype(bf16)

    pl.semaphore_wait(barrier, n_chan - 1 + n_tm - 1 + ROW - 1)

    halo = pltpu.make_async_remote_copy(
        src_ref=seis.at[:, pl.ds(0, HALO * LANES)], dst_ref=halo_in,
        send_sem=sems.at[0], recv_sem=sems.at[1],
        device_id=(me, jnp.maximum(now - 1, 0)), device_id_type=MESH,
    )

    sends_part = across < WAVE_BLOCKS
    block_of = jnp.minimum(across, WAVE_BLOCKS - 1)

    def part(half):
        return normed.at[pl.ds(half * 16, 16), pl.ds(block_of * LANES, LANES)]

    def part_copy(peer):
        return pltpu.make_async_remote_copy(
            src_ref=part(lax.rem(peer, HALVES)), dst_ref=part_in.at[me],
            send_sem=sems.at[2], recv_sem=sems.at[3],
            device_id=(peer, now), device_id_type=MESH,
        )

    @pl.when(sends_part)
    def _():
        for peer in chan_peers:
            part_copy(peer).start()

    @pl.when(now > 0)
    def _():
        halo.start()

    loads[1].wait()
    loads[2].wait()
    templates, per_template = listed_in.shape
    names = listed_in[...]
    column = lax.broadcasted_iota(i32, names.shape, 1)
    key = jnp.full(names.shape, -1, i32)
    code = (lax.broadcasted_iota(i32, names.shape, 0) * 32 + column) * LANES + moves_in[...]
    counts = jnp.zeros((templates, 1), i32)
    for place, group in ((0, me), (SEL, sibling)):
        from_first = names - group * channels
        inside = (from_first >= 0) & (from_first < channels)
        mine = jnp.where(inside, 1, 0)
        in_row = before(mine, 1)
        full_row = jnp.sum(mine, axis=1, keepdims=True)
        rank = in_row + before(jnp.broadcast_to(full_row, mine.shape), 0)
        key = jnp.where(inside & (rank < SLOTS), rank + place, key)
        code = jnp.where(inside, code + from_first * (1 << 17), code)
        if place == 0:
            counts = full_row
    lane32 = lax.broadcasted_iota(i32, (templates, LANES), 1)
    found = jnp.zeros((templates, LANES), i32)
    for c in range(per_template):
        found = found + jnp.where(
            lane32 == jnp.broadcast_to(key[:, c : c + 1], lane32.shape),
            jnp.broadcast_to(code[:, c : c + 1], lane32.shape), 0,
        )
    ahead = jnp.where(
        lax.broadcasted_iota(i32, lane32.shape, 0) < lane32, jnp.broadcast_to(counts, lane32.shape), 0
    )
    tab_v[0:1, :] = jnp.sum(found, axis=0, keepdims=True)
    tab_v[1:2, :] = jnp.minimum(jnp.sum(ahead, axis=0, keepdims=True), SLOTS)
    to_scalars = pltpu.make_async_copy(tab_v, tab, in_sems.at[4])
    to_scalars.start()

    def lay(ref, first):
        for i in range(ref.shape[1] // LANES):
            for c in range(0, channels, 16):
                flat_rows[pl.ds(c * pitch + first + i, 16, stride=pitch), :] = ref[
                    c : c + 16, i * LANES : (i + 1) * LANES
                ].astype(f32)

    loads[3].wait()
    lay(x_in, 0)
    to_scalars.wait()

    def template_of(code):
        return (code >> 12) & 31

    def row_of(code):
        return (code >> 7) & 31

    lane = lax.broadcasted_iota(i32, (half_tiles, LANES), 1)
    left = lane < HALF_LANES
    together = 4

    def prepare(group, half):
        squares = []
        first = half * half_tiles
        for u in range(together):
            station = group * together + u
            for d in range(PER):
                entry = tab[0, station * PER + d]
                move = entry & (LANES - 1)
                record = rows[entry >> 17][first : first + half_tiles + 8]
                at = u * PER + d
                turned[at] = pltpu.roll(record, lax.rem(LANES - move, LANES), 1)
                here = lane < LANES - move
                parts = [turned[at, b : b + half_tiles, :] for b in range(BLOCKS + 1)]
                shifted = [jnp.where(here, parts[b], parts[b + 1]) for b in range(BLOCKS)]
                swung = [pltpu.roll(s, HALF_LANES, 1) for s in shifted]
                later = [jnp.where(left, swung[b], swung[b + 1]) for b in range(WAVE_BLOCKS)]
                for phase, tile in enumerate((shifted[:WAVE_BLOCKS], later)):
                    at_row = (at % 2 * 2 + phase) * tiles + first
                    lhs[group * (together * PER // 2) + at // 2, at_row : at_row + half_tiles, :] = jnp.concatenate(
                        [s.astype(bf16) for s in tile], axis=1
                    )
                squares.append(jnp.concatenate([(s * s).astype(bf16) for s in shifted], axis=1))
        energy = jnp.dot(jnp.concatenate(squares, axis=0), band[...], preferred_element_type=f32)
        factor = lax.rsqrt(energy / length + EPS) / math.sqrt(length)
        for u in range(together):
            for d in range(PER):
                at = (u * PER + d) * half_tiles
                scale[group * together + u, d, first : first + half_tiles, :] = factor[at : at + half_tiles]

    each(STATIONS // together, lambda g: prepare(g, 0))

    def chosen_copy(other, d):
        return pltpu.make_async_remote_copy(
            src_ref=chosen.at[other], dst_ref=chosen_in.at[block_of * HALVES + core],
            send_sem=sems.at[4], recv_sem=sems.at[5],
            device_id=(sibling if other else me, row_peer(d)), device_id_type=MESH,
        )

    @pl.when(sends_part)
    def _():
        wait_for(part_in, n_chan - 1, sems.at[3])
        part_all[pl.ds(me * 16, 16), :] = part(core)[...].astype(f32)

        for peer in chan_peers:
            part_all[pl.ds(peer * 16, 16), :] = part_in[peer].astype(f32)
        for other in (1, 0):
            picks = []
            for k in range(SLOTS):
                entry = tab[0, other * SEL + k]
                at = template_of(entry) * 16 + (row_of(entry) & 15)
                picks.append(part_all[at].reshape(1, LANES))
            for k in range(SLOTS, SEL):
                picks.append(jnp.zeros((1, LANES), f32))
            chosen[other] = jnp.concatenate(picks, axis=0).astype(bf16)
            if other:
                chosen_copy(1, 0).start()
            for d in (2, 1, 3):
                chosen_copy(other, d).start()

    @pl.when(now < n_tm - 1)
    def _():
        halo.wait_recv()

    @pl.when(now == n_tm - 1)
    def _():
        halo_in[...] = jnp.zeros_like(halo_in)

    lay(halo_in, tiles)
    each(STATIONS // together, lambda g: prepare(g, 1))

    @pl.when(sends_part)
    def _():
        wait_for(chosen_in, PARTS - 1, sems.at[5])

    @pl.when(jnp.logical_not(sends_part))
    def _():
        wait_for(chosen_in, PARTS, sems.at[5])

    for p in range(PARTS):
        own = sends_part & (block_of * HALVES + core == p)

        @pl.when(own)
        def _():
            chosen_all[p * SEL : (p + 1) * SEL, :] = chosen[0].astype(f32)

        @pl.when(jnp.logical_not(own))
        def _():
            chosen_all[p * SEL : (p + 1) * SEL, :] = chosen_in[p].astype(f32)

    running[0] = jnp.zeros((tiles, LANES), f32)

    at_once = 20
    left_all = lax.broadcasted_iota(i32, (tiles, LANES), 1) < HALF_LANES

    def toeplitz_of(k):
        half = row_of(tab[0, k]) >> 4
        wave = [chosen_all[(HALVES * b + half) * SEL + k].reshape(1, LANES) for b in range(WAVE_BLOCKS)]
        wide = jnp.broadcast_to(jnp.concatenate(wave, axis=1), (HALF_LANES, WAVE_BLOCKS * LANES))
        return pltpu.roll(wide, 0, 1, stride=1, stride_axis=0).astype(bf16)

    def correlate(group, total):
        numers = []
        for p in range(at_once * PER // 2):
            pair = group * (at_once * PER // 2) + p
            both = lax.dot_general(
                lhs[pair], jnp.concatenate([toeplitz_of(pair * 2), toeplitz_of(pair * 2 + 1)], axis=0),
                (((1,), (1,)), ((), ())), preferred_element_type=f32,
            )
            first, second, third, fourth = (both[i * tiles : (i + 1) * tiles] for i in range(4))
            swapped = pltpu.roll(jnp.where(left_all, second, third), HALF_LANES, 1)
            numers.append(jnp.where(left_all, first, swapped))
            numers.append(jnp.where(left_all, swapped, fourth))
        for u in range(at_once):
            station = group * at_once + u
            for d in range(PER):
                total = total + numers[u * PER + d] * scale[station, d]
            running[station + 1] = total
        return total

    lax.fori_loop(0, STATIONS // at_once, correlate, jnp.zeros((tiles, LANES), f32))

    def summed(template):
        return running[tab[1, template + 1] // PER] - running[tab[1, template] // PER]

    pair = pltpu.make_async_remote_copy(
        src_ref=pair_out, dst_ref=pair_in, send_sem=sems.at[10], recv_sem=sems.at[11],
        device_id=(sibling, now), device_id_type=MESH,
    )
    for i in range(n_chan // HALVES):
        pair_out[i] = summed(i * HALVES + 1 - core)
    pair.start()

    def stack_copy(place):
        return pltpu.make_async_remote_copy(
            src_ref=outgoing.at[place], dst_ref=incoming.at[chip],
            send_sem=sems.at[6], recv_sem=sems.at[7],
            device_id=(place * HALVES + core, now), device_id_type=MESH,
        )

    pair.wait_recv()
    for place in far_chips:
        outgoing[place] = (summed(place * HALVES + core) + pair_in[place]).astype(bf16)
        stack_copy(place).start()
    stack = summed(me) + pair_in[chip]
    if far_chips:
        wait_for(incoming, len(far_chips), sems.at[7])
    for place in far_chips:
        stack = stack + incoming[place].astype(f32)
    stack_out[...] = stack
    peak_mine[...] = jnp.max(jnp.abs(stack).reshape(tiles // 8, 8, LANES), axis=0)

    def peak_copy(i):
        return pltpu.make_async_remote_copy(
            src_ref=peak_mine, dst_ref=peak_in.at[now],
            send_sem=sems.at[8], recv_sem=sems.at[9],
            device_id=(me, tm_peer(i + 1)), device_id_type=MESH,
        )

    for i in range(n_tm - 1):
        peak_copy(i).start()
    wait_for(peak_in, n_tm - 1, sems.at[9])
    peak = peak_mine[...]
    for i in range(n_tm - 1):
        peak = jnp.maximum(peak, peak_in[tm_peer(i + 1)])
    peak_out[...] = peak

    @pl.when(now > 0)
    def _():
        halo.wait_send()

    @pl.when(sends_part)
    def _():
        wait_for(part_in, n_chan - 1, sems.at[2])
        wait_for(chosen_in, 2 * ROW - 1, sems.at[4])

    pair.wait_send()
    if far_chips:
        wait_for(outgoing, len(far_chips), sems.at[6])
    wait_for(peak_in, n_tm - 1, sems.at[8])


def on_device(n_chan, n_tm, seismic, waveforms, channel_list, moveouts):
    channels, piece = seismic.shape
    length = waveforms.shape[2]
    tiles = piece // LANES
    pitch = tiles + 8
    f32, bf16, i32 = jnp.float32, jnp.bfloat16, jnp.int32
    stack, peak = pl.pallas_call(
        functools.partial(kernel, n_chan, n_tm, length, channels),
        out_shape=(
            jax.ShapeDtypeStruct((tiles, LANES), f32),
            jax.ShapeDtypeStruct((8, LANES), f32),
        ),
        in_specs=[pl.BlockSpec(memory_space=pltpu.HBM)] * 4,
        out_specs=[pl.BlockSpec(memory_space=pltpu.VMEM)] * 2,
        scratch_shapes=[
            pltpu.VMEM(channel_list.shape, i32),
            pltpu.VMEM(moveouts.shape, i32),
            pltpu.VMEM((waveforms.shape[1], 1, length), f32),
            pltpu.VMEM((channels, piece), bf16),
            pltpu.VMEM((channels, HALO * LANES), bf16),
            pltpu.VMEM((8, LANES), i32),
            pltpu.SMEM((8, LANES), i32),
            pltpu.VMEM((channels, pitch, LANES), f32),
            pltpu.VMEM((4 * PER, tiles // 2 + 8, LANES), f32),
            pltpu.VMEM((SLOTS // 2, 4 * tiles, WAVE_BLOCKS * LANES), bf16),
            pltpu.VMEM((STATIONS, PER, tiles, LANES), f32),
            pltpu.VMEM((BLOCKS * LANES, LANES), bf16),
            pltpu.VMEM((32, WAVE_BLOCKS * LANES), bf16),
            pltpu.VMEM((n_chan, 16, LANES), bf16),
            pltpu.VMEM((n_chan * 16, LANES), f32),
            pltpu.VMEM((2, SEL, LANES), bf16),
            pltpu.VMEM((2 * ROW, SEL, LANES), bf16),
            pltpu.VMEM((PARTS * SEL, LANES), f32),
            pltpu.VMEM((STATIONS + 1, tiles, LANES), f32),
            pltpu.VMEM((n_chan // HALVES, tiles, LANES), f32),
            pltpu.VMEM((n_chan // HALVES, tiles, LANES), f32),
            pltpu.VMEM((n_chan // HALVES, tiles, LANES), bf16),
            pltpu.VMEM((n_chan // HALVES, tiles, LANES), bf16),
            pltpu.VMEM((8, LANES), f32),
            pltpu.VMEM((n_tm, 8, LANES), f32),
            pltpu.SemaphoreType.DMA((12,)),
            pltpu.SemaphoreType.DMA((5,)),
        ],
        compiler_params=pltpu.CompilerParams(
            collective_id=0, has_side_effects=True, vmem_limit_bytes=GRANT
        ),
    )(channel_list, moveouts, seismic, jnp.transpose(waveforms, (1, 0, 2)))
    return stack.reshape(1, piece), jnp.max(peak).reshape(1)


def solution(mesh):
    return jax.shard_map(
        functools.partial(on_device, mesh.shape["chan"], mesh.shape["tm"]),
        mesh=mesh,
        in_specs=(P("chan", "tm"), P("chan", None, None), P(), P()),
        out_specs=(P("chan", "tm"), P("chan")),
        check_vma=False,
    )
```

```python
import functools
import math

import jax
import jax.numpy as jnp
from jax import lax
from jax.experimental import pallas as pl
from jax.experimental.pallas import tpu as pltpu
from jax.sharding import PartitionSpec as P

LANES = 128
HALF_LANES = 64
STATIONS = 20
PER = 3
SLOTS = STATIONS * PER
SEL = 64
HALO = 4
BLOCKS = 4
WAVE_BLOCKS = 3
HALVES = 2
PARTS = WAVE_BLOCKS * HALVES
ROW = 4
RING = 8
PAIR_PIECES = 2
EPS = 1e-05
GRANT = 55200 * 1024
MESH = pl.DeviceIdType.MESH


def each(count, body, unroll=1):
    def step(i, carry):
        for u in range(unroll):
            body(i * unroll + u)
        return carry

    assert count % unroll == 0
    lax.fori_loop(0, count // unroll, step, 0)


def ring_offsets(n_chan):
    chips = n_chan // HALVES
    depth = min(RING, chips)
    offsets = [(dy, dz) for dy in range(chips // depth) for dz in range(depth)]
    return sorted(offsets, key=lambda o: (-(o[0] + min(o[1], depth - o[1])), o))


def before(x, axis):
    index = lax.broadcasted_iota(jnp.int32, x.shape, axis)
    step, total = 1, x
    while step < 32:
        total = total + jnp.where(index >= step, pltpu.roll(total, step, axis), 0)
        step *= 2
    return total - x


def kernel(
    n_chan, n_tm, length, channels,
    listed, moves, seis, waves,
    stack_out, peak_out,
    listed_in, moves_in, waves_in, x_in, halo_in, tab_v, tab,
    rows, turned, lhs, scale, band,
    normed, part_in, takes, chosen, chosen_in, chosen_all,
    running, mine_out, pair_out, pair_in, outgoing, incoming, peak_mine, peak_in,
    sems, pair_sems, in_sems,
):
    me = lax.axis_index("chan")
    now = lax.axis_index("tm")
    core = lax.rem(me, HALVES)
    across = lax.rem(now, ROW)
    row_start = now - across
    sibling = me + 1 - 2 * core
    tiles = stack_out.shape[0]
    pitch = rows.shape[1]
    flat_rows = rows.reshape(channels * pitch, LANES)
    half_tiles = tiles // 2
    f32, bf16, i32 = jnp.float32, jnp.bfloat16, jnp.int32

    def wait_for(ref, blocks, sem):
        span = ref.at[pl.ds(0, blocks)]
        pltpu.make_async_copy(span, span, sem).wait()

    chip = me // HALVES
    depth = min(RING, n_chan // HALVES)
    offsets = ring_offsets(n_chan)

    def chip_at(offset):
        dy, dz = offset
        y, z = chip // depth, lax.rem(chip, depth)
        return lax.rem(y + dy, n_chan // HALVES // depth) * depth + lax.rem(z + dz, depth)

    chan_peers = [
        chip_at(offset) * HALVES + lax.rem(core + dc, HALVES)
        for offset in offsets for dc in range(HALVES) if offset != (0, 0) or dc
    ]
    far_chips = [chip_at(offset) for offset in offsets if offset != (0, 0)]

    def tm_peer(d):
        return lax.rem(now + d, n_tm)

    def row_peer(d):
        return row_start + lax.rem(across + d, ROW)

    barrier = pltpu.get_barrier_semaphore()

    loads = [
        pltpu.make_async_copy(src, dst, in_sems.at[i])
        for i, (src, dst) in enumerate(
            ((waves, waves_in), (listed, listed_in), (moves, moves_in), (seis, x_in))
        )
    ]
    loads[0].start()

    def greet(group, piece):
        pl.semaphore_signal(barrier, inc=1, device_id=(group, piece), device_id_type=MESH)

    for peer in chan_peers[: n_chan // 2]:
        greet(peer, now)
    for i in range(n_tm - 1):
        greet(me, tm_peer(i + 1))
    for i in range(ROW - 1):
        greet(sibling, row_peer(i + 1))
    for peer in chan_peers[n_chan // 2 :]:
        greet(peer, now)

    for copy in loads[1:]:
        copy.start()

    loads[0].wait()
    w = waves_in[:, 0, :]
    centered = w - jnp.mean(w, axis=-1, keepdims=True)
    factor = lax.rsqrt(jnp.mean(centered * centered, axis=-1, keepdims=True) + EPS) / math.sqrt(length)
    normed[...] = jnp.zeros_like(normed)
    normed[0 : w.shape[0], 0:length] = (centered * factor).astype(bf16)

    pl.semaphore_wait(barrier, n_chan - 1 + n_tm - 1 + ROW - 1)

    halo = pltpu.make_async_remote_copy(
        src_ref=seis.at[:, pl.ds(0, HALO * LANES)], dst_ref=halo_in,
        send_sem=sems.at[0], recv_sem=sems.at[1],
        device_id=(me, jnp.maximum(now - 1, 0)), device_id_type=MESH,
    )

    sends_part = across < WAVE_BLOCKS
    block_of = jnp.minimum(across, WAVE_BLOCKS - 1)

    def part(half):
        return normed.at[pl.ds(half * 16, 16), pl.ds(block_of * LANES, LANES)]

    def part_copy(peer):
        return pltpu.make_async_remote_copy(
            src_ref=part(lax.rem(peer, HALVES)), dst_ref=part_in.at[me],
            send_sem=sems.at[2], recv_sem=sems.at[3],
            device_id=(peer, now), device_id_type=MESH,
        )

    @pl.when(sends_part)
    def _():
        for peer in chan_peers:
            part_copy(peer).start()
        part_in[me] = part(core)[...]

    @pl.when(now > 0)
    def _():
        halo.start()

    lag = lax.broadcasted_iota(i32, band.shape, 0) - lax.broadcasted_iota(i32, band.shape, 1)
    band[...] = jnp.where((lag >= 0) & (lag < length), 1.0, 0.0).astype(bf16)

    loads[1].wait()
    loads[2].wait()
    templates, per_template = listed_in.shape
    names = listed_in[...]
    column = lax.broadcasted_iota(i32, names.shape, 1)
    key = jnp.full(names.shape, -1, i32)
    code = (lax.broadcasted_iota(i32, names.shape, 0) * 32 + column) * LANES + moves_in[...]
    counts = jnp.zeros((templates, 1), i32)
    for place, group in ((0, me), (SEL, sibling)):
        from_first = names - group * channels
        inside = (from_first >= 0) & (from_first < channels)
        mine = jnp.where(inside, 1, 0)
        in_row = before(mine, 1)
        full_row = jnp.sum(mine, axis=1, keepdims=True)
        rank = in_row + before(jnp.broadcast_to(full_row, mine.shape), 0)
        key = jnp.where(inside & (rank < SLOTS), rank + place, key)
        code = jnp.where(inside, code + from_first * (1 << 17), code)
        if place == 0:
            counts = full_row
    lane32 = lax.broadcasted_iota(i32, (templates, LANES), 1)
    found = jnp.zeros((templates, LANES), i32)
    for c in range(per_template):
        found = found + jnp.where(
            lane32 == jnp.broadcast_to(key[:, c : c + 1], lane32.shape),
            jnp.broadcast_to(code[:, c : c + 1], lane32.shape), 0,
        )
    ahead = jnp.where(
        lax.broadcasted_iota(i32, lane32.shape, 0) < lane32, jnp.broadcast_to(counts, lane32.shape), 0
    )
    tab_v[0:1, :] = jnp.sum(found, axis=0, keepdims=True)
    tab_v[1:2, :] = jnp.minimum(jnp.sum(ahead, axis=0, keepdims=True), SLOTS)
    to_scalars = pltpu.make_async_copy(tab_v, tab, in_sems.at[4])
    to_scalars.start()

    def lay(ref, first):
        for i in range(ref.shape[1] // LANES):
            for c in range(0, channels, 16):
                flat_rows[pl.ds(c * pitch + first + i, 16, stride=pitch), :] = ref[
                    c : c + 16, i * LANES : (i + 1) * LANES
                ].astype(f32)

    loads[3].wait()
    lay(x_in, 0)
    to_scalars.wait()

    entries = tab_v[0:1, :]
    rows_of = (entries >> 7) & 31
    taken = jnp.where(rows_of // 16 == core, ((entries >> 12) & 31) * 16 + rows_of % 16, -1)
    taken = jnp.broadcast_to(taken, (n_chan * 16, LANES))
    hot = jnp.where(lax.broadcasted_iota(i32, taken.shape, 0) == taken, 1.0, 0.0)
    for b in range(n_chan * 16 // LANES):
        takes[:, b * LANES : (b + 1) * LANES] = hot[b * LANES : (b + 1) * LANES].T.astype(bf16)

    lane = lax.broadcasted_iota(i32, (half_tiles, LANES), 1)
    left = lane < HALF_LANES
    together = 4

    def prepare(group, half):
        squares = []
        first = half * half_tiles
        for u in range(together):
            station = group * together + u
            for d in range(PER):
                entry = tab[0, station * PER + d]
                move = entry & (LANES - 1)
                record = rows[entry >> 17][first : first + half_tiles + 8]
                at = u * PER + d
                turned[at] = pltpu.roll(record, lax.rem(LANES - move, LANES), 1)
                here = lane < LANES - move
                parts = [turned[at, b : b + half_tiles, :] for b in range(BLOCKS + 1)]
                shifted = [jnp.where(here, parts[b], parts[b + 1]) for b in range(BLOCKS)]
                swung = [pltpu.roll(s, HALF_LANES, 1) for s in shifted]
                later = [jnp.where(left, swung[b], swung[b + 1]) for b in range(WAVE_BLOCKS)]
                for phase, tile in enumerate((shifted[:WAVE_BLOCKS], later)):
                    at_row = (at % 2 * 2 + phase) * tiles + first
                    lhs[group * (together * PER // 2) + at // 2, at_row : at_row + half_tiles, :] = jnp.concatenate(
                        [s.astype(bf16) for s in tile], axis=1
                    )
                squares.append(jnp.concatenate([(s * s).astype(bf16) for s in shifted], axis=1))
        energy = jnp.dot(jnp.concatenate(squares, axis=0), band[...], preferred_element_type=f32)
        factor = lax.rsqrt(energy / length + EPS) / math.sqrt(length)
        for u in range(together):
            for d in range(PER):
                at = (u * PER + d) * half_tiles
                scale[group * together + u, d, first : first + half_tiles, :] = factor[at : at + half_tiles]

    each(STATIONS // together, lambda g: prepare(g, 0))

    def chosen_copy(other, d):
        return pltpu.make_async_remote_copy(
            src_ref=chosen.at[other], dst_ref=chosen_in.at[block_of * HALVES + core],
            send_sem=sems.at[4], recv_sem=sems.at[5],
            device_id=(sibling if other else me, row_peer(d)), device_id_type=MESH,
        )

    @pl.when(sends_part)
    def _():
        wait_for(part_in, n_chan - 1, sems.at[3])
        picked = jnp.dot(
            takes[...], part_in[...].reshape(n_chan * 16, LANES), preferred_element_type=f32
        ).astype(bf16)
        for other in (1, 0):
            chosen[other] = picked[other * SEL : (other + 1) * SEL]
            if other:
                chosen_copy(1, 0).start()
            for d in (2, 1, 3):
                chosen_copy(other, d).start()

    @pl.when(now < n_tm - 1)
    def _():
        halo.wait_recv()

    @pl.when(now == n_tm - 1)
    def _():
        halo_in[...] = jnp.zeros_like(halo_in)

    lay(halo_in, tiles)
    each(STATIONS // together, lambda g: prepare(g, 1))

    @pl.when(sends_part)
    def _():
        wait_for(chosen_in, PARTS - 1, sems.at[5])

    @pl.when(jnp.logical_not(sends_part))
    def _():
        wait_for(chosen_in, PARTS, sems.at[5])

    for p in range(PARTS):
        own = sends_part & (block_of * HALVES + core == p)

        @pl.when(own)
        def _():
            chosen_in[p] = chosen[0]

    for b in range(WAVE_BLOCKS):
        halves = [chosen_in[b * HALVES + h].astype(f32) for h in range(HALVES)]
        chosen_all[:, b * LANES : (b + 1) * LANES] = halves[0] + halves[1]

    running[0] = jnp.zeros((tiles, LANES), f32)

    at_once = 20
    left_all = lax.broadcasted_iota(i32, (tiles, LANES), 1) < HALF_LANES

    def toeplitz_of(k):
        wide = jnp.broadcast_to(chosen_all[pl.ds(k, 1), :], (HALF_LANES, WAVE_BLOCKS * LANES))
        return pltpu.roll(wide, 0, 1, stride=1, stride_axis=0).astype(bf16)

    def correlate(group, total):
        numers = []
        for p in range(at_once * PER // 2):
            pair = group * (at_once * PER // 2) + p
            both = lax.dot_general(
                lhs[pair], jnp.concatenate([toeplitz_of(pair * 2), toeplitz_of(pair * 2 + 1)], axis=0),
                (((1,), (1,)), ((), ())), preferred_element_type=f32,
            )
            first, second, third, fourth = (both[i * tiles : (i + 1) * tiles] for i in range(4))
            swapped = pltpu.roll(jnp.where(left_all, second, third), HALF_LANES, 1)
            numers.append(jnp.where(left_all, first, swapped))
            numers.append(jnp.where(left_all, swapped, fourth))
        for u in range(at_once):
            station = group * at_once + u
            for d in range(PER):
                total = total + numers[u * PER + d] * scale[station, d]
            running[station + 1] = total
        return total

    lax.fori_loop(0, STATIONS // at_once, correlate, jnp.zeros((tiles, LANES), f32))

    def summed(template):
        return running[tab[1, template + 1] // PER] - running[tab[1, template] // PER]

    places = far_chips + [chip]
    share = len(places) // PAIR_PIECES

    def pair_copy(piece):
        span = pl.ds(piece * share, share)
        return pltpu.make_async_remote_copy(
            src_ref=pair_out.at[span], dst_ref=pair_in.at[span],
            send_sem=pair_sems.at[0, piece], recv_sem=pair_sems.at[1, piece],
            device_id=(sibling, now), device_id_type=MESH,
        )

    for piece in range(PAIR_PIECES):
        for i in range(piece * share, (piece + 1) * share):
            pair_out[i] = summed(places[i] * HALVES + 1 - core)
        pair_copy(piece).start()

    def stack_copy(place):
        return pltpu.make_async_remote_copy(
            src_ref=outgoing.at[place], dst_ref=incoming.at[chip],
            send_sem=sems.at[6], recv_sem=sems.at[7],
            device_id=(place * HALVES + core, now), device_id_type=MESH,
        )

    for i, place in enumerate(places):
        mine_out[i] = summed(place * HALVES + core)
    stack = jnp.zeros((tiles, LANES), f32)
    for i, place in enumerate(places):
        if i % share == 0:
            pair_copy(i // share).wait_recv()
        stack = mine_out[i] + pair_in[i]
        if i < len(far_chips):
            outgoing[place] = stack.astype(bf16)
            stack_copy(place).start()
    if far_chips:
        wait_for(incoming, len(far_chips), sems.at[7])
    for place in far_chips:
        stack = stack + incoming[place].astype(f32)
    stack_out[...] = stack
    peak_mine[...] = jnp.max(jnp.abs(stack).reshape(tiles // 8, 8, LANES), axis=0)

    def peak_copy(i):
        return pltpu.make_async_remote_copy(
            src_ref=peak_mine, dst_ref=peak_in.at[now],
            send_sem=sems.at[8], recv_sem=sems.at[9],
            device_id=(me, tm_peer(i + 1)), device_id_type=MESH,
        )

    for i in range(n_tm - 1):
        peak_copy(i).start()
    wait_for(peak_in, n_tm - 1, sems.at[9])
    peak = peak_mine[...]
    for i in range(n_tm - 1):
        peak = jnp.maximum(peak, peak_in[tm_peer(i + 1)])
    peak_out[...] = peak

    @pl.when(now > 0)
    def _():
        halo.wait_send()

    @pl.when(sends_part)
    def _():
        wait_for(part_in, n_chan - 1, sems.at[2])
        wait_for(chosen_in, 2 * ROW - 1, sems.at[4])

    for piece in range(PAIR_PIECES):
        pair_copy(piece).wait_send()
    if far_chips:
        wait_for(outgoing, len(far_chips), sems.at[6])
    wait_for(peak_in, n_tm - 1, sems.at[8])


def on_device(n_chan, n_tm, seismic, waveforms, channel_list, moveouts):
    channels, piece = seismic.shape
    length = waveforms.shape[2]
    tiles = piece // LANES
    pitch = tiles + 8
    f32, bf16, i32 = jnp.float32, jnp.bfloat16, jnp.int32
    stack, peak = pl.pallas_call(
        functools.partial(kernel, n_chan, n_tm, length, channels),
        out_shape=(
            jax.ShapeDtypeStruct((tiles, LANES), f32),
            jax.ShapeDtypeStruct((8, LANES), f32),
        ),
        in_specs=[pl.BlockSpec(memory_space=pltpu.HBM)] * 4,
        out_specs=[pl.BlockSpec(memory_space=pltpu.VMEM)] * 2,
        scratch_shapes=[
            pltpu.VMEM(channel_list.shape, i32),
            pltpu.VMEM(moveouts.shape, i32),
            pltpu.VMEM((waveforms.shape[1], 1, length), f32),
            pltpu.VMEM((channels, piece), bf16),
            pltpu.VMEM((channels, HALO * LANES), bf16),
            pltpu.VMEM((8, LANES), i32),
            pltpu.SMEM((8, LANES), i32),
            pltpu.VMEM((channels, pitch, LANES), f32),
            pltpu.VMEM((4 * PER, tiles // 2 + 8, LANES), f32),
            pltpu.VMEM((SLOTS // 2, 4 * tiles, WAVE_BLOCKS * LANES), bf16),
            pltpu.VMEM((STATIONS, PER, tiles, LANES), f32),
            pltpu.VMEM((BLOCKS * LANES, LANES), bf16),
            pltpu.VMEM((32, WAVE_BLOCKS * LANES), bf16),
            pltpu.VMEM((n_chan, 16, LANES), bf16),
            pltpu.VMEM((2 * SEL, n_chan * 16), bf16),
            pltpu.VMEM((2, SEL, LANES), bf16),
            pltpu.VMEM((2 * ROW, SEL, LANES), bf16),
            pltpu.VMEM((SEL, WAVE_BLOCKS * LANES), f32),
            pltpu.VMEM((STATIONS + 1, tiles, LANES), f32),
            pltpu.VMEM((n_chan // HALVES, tiles, LANES), f32),
            pltpu.VMEM((n_chan // HALVES, tiles, LANES), f32),
            pltpu.VMEM((n_chan // HALVES, tiles, LANES), f32),
            pltpu.VMEM((n_chan // HALVES, tiles, LANES), bf16),
            pltpu.VMEM((n_chan // HALVES, tiles, LANES), bf16),
            pltpu.VMEM((8, LANES), f32),
            pltpu.VMEM((n_tm, 8, LANES), f32),
            pltpu.SemaphoreType.DMA((10,)),
            pltpu.SemaphoreType.DMA((2, PAIR_PIECES)),
            pltpu.SemaphoreType.DMA((5,)),
        ],
        compiler_params=pltpu.CompilerParams(
            collective_id=0, has_side_effects=True, vmem_limit_bytes=GRANT
        ),
    )(channel_list, moveouts, seismic, jnp.transpose(waveforms, (1, 0, 2)))
    return stack.reshape(1, piece), jnp.max(peak).reshape(1)


def solution(mesh):
    return jax.shard_map(
        functools.partial(on_device, mesh.shape["chan"], mesh.shape["tm"]),
        mesh=mesh,
        in_specs=(P("chan", "tm"), P("chan", None, None), P(), P()),
        out_specs=(P("chan", "tm"), P("chan")),
        check_vma=False,
    )
```

```python
import functools
import math

import jax
import jax.numpy as jnp
from jax import lax
from jax.experimental import pallas as pl
from jax.experimental.pallas import tpu as pltpu
from jax.sharding import PartitionSpec as P

LANES = 128
HALF_LANES = 64
STATIONS = 20
PER = 3
SLOTS = STATIONS * PER
SEL = 64
HALO = 4
BLOCKS = 4
WAVE_BLOCKS = 3
HALVES = 2
PARTS = WAVE_BLOCKS * HALVES
ROW = 4
RING = 8
PAIR_PIECES = 2
EPS = 1e-05
GRANT = 55200 * 1024
MESH = pl.DeviceIdType.MESH


def each(count, body, unroll=1):
    def step(i, carry):
        for u in range(unroll):
            body(i * unroll + u)
        return carry

    assert count % unroll == 0
    lax.fori_loop(0, count // unroll, step, 0)


def ring_offsets(n_chan):
    chips = n_chan // HALVES
    depth = min(RING, chips)
    offsets = [(dy, dz) for dy in range(chips // depth) for dz in range(depth)]
    return sorted(offsets, key=lambda o: (-(o[0] + min(o[1], depth - o[1])), o))


def before(x, axis):
    index = lax.broadcasted_iota(jnp.int32, x.shape, axis)
    step, total = 1, x
    while step < 32:
        total = total + jnp.where(index >= step, pltpu.roll(total, step, axis), 0)
        step *= 2
    return total - x


def kernel(
    n_chan, n_tm, length, channels,
    listed, moves, seis, waves,
    stack_out, peak_out,
    listed_in, moves_in, waves_in, x_in, halo_in, tab_v, tab,
    rows, turned, lhs, scale, band,
    normed, part_in, takes, chosen, chosen_in, chosen_all,
    running, mine_out, pair_out, pair_in, outgoing, incoming, peak_mine, peak_in,
    sems, pair_sems, in_sems,
):
    me = lax.axis_index("chan")
    now = lax.axis_index("tm")
    core = lax.rem(me, HALVES)
    across = lax.rem(now, ROW)
    row_start = now - across
    sibling = me + 1 - 2 * core
    tiles = stack_out.shape[0]
    pitch = rows.shape[1]
    flat_rows = rows.reshape(channels * pitch, LANES)
    half_tiles = tiles // 2
    f32, bf16, i32 = jnp.float32, jnp.bfloat16, jnp.int32

    def wait_for(ref, blocks, sem):
        span = ref.at[pl.ds(0, blocks)]
        pltpu.make_async_copy(span, span, sem).wait()

    chip = me // HALVES
    depth = min(RING, n_chan // HALVES)
    offsets = ring_offsets(n_chan)

    def chip_at(offset):
        dy, dz = offset
        y, z = chip // depth, lax.rem(chip, depth)
        return lax.rem(y + dy, n_chan // HALVES // depth) * depth + lax.rem(z + dz, depth)

    chan_peers = [
        chip_at(offset) * HALVES + lax.rem(core + dc, HALVES)
        for offset in offsets for dc in range(HALVES) if offset != (0, 0) or dc
    ]
    far_chips = [chip_at(offset) for offset in offsets if offset != (0, 0)]

    def tm_peer(d):
        return lax.rem(now + d, n_tm)

    def row_peer(d):
        return row_start + lax.rem(across + d, ROW)

    barrier = pltpu.get_barrier_semaphore()

    loads = [
        pltpu.make_async_copy(src, dst, in_sems.at[i])
        for i, (src, dst) in enumerate(
            ((waves, waves_in), (listed, listed_in), (moves, moves_in), (seis, x_in))
        )
    ]
    loads[0].start()

    def greet(group, piece):
        pl.semaphore_signal(barrier, inc=1, device_id=(group, piece), device_id_type=MESH)

    for peer in chan_peers[: n_chan // 2]:
        greet(peer, now)
    for i in range(n_tm - 1):
        greet(me, tm_peer(i + 1))
    for i in range(ROW - 1):
        greet(sibling, row_peer(i + 1))
    for peer in chan_peers[n_chan // 2 :]:
        greet(peer, now)

    for copy in loads[1:]:
        copy.start()

    loads[0].wait()
    w = waves_in[:, 0, :]
    centered = w - jnp.mean(w, axis=-1, keepdims=True)
    factor = lax.rsqrt(jnp.mean(centered * centered, axis=-1, keepdims=True) + EPS) / math.sqrt(length)
    normed[...] = jnp.zeros_like(normed)
    normed[0 : w.shape[0], 0:length] = (centered * factor).astype(bf16)

    pl.semaphore_wait(barrier, n_chan - 1 + n_tm - 1 + ROW - 1)

    halo = pltpu.make_async_remote_copy(
        src_ref=seis.at[:, pl.ds(0, HALO * LANES)], dst_ref=halo_in,
        send_sem=sems.at[0], recv_sem=sems.at[1],
        device_id=(me, jnp.maximum(now - 1, 0)), device_id_type=MESH,
    )

    sends_part = across < WAVE_BLOCKS
    block_of = jnp.minimum(across, WAVE_BLOCKS - 1)

    def part(half):
        return normed.at[pl.ds(half * 16, 16), pl.ds(block_of * LANES, LANES)]

    def part_copy(peer):
        return pltpu.make_async_remote_copy(
            src_ref=part(lax.rem(peer, HALVES)), dst_ref=part_in.at[me],
            send_sem=sems.at[2], recv_sem=sems.at[3],
            device_id=(peer, now), device_id_type=MESH,
        )

    @pl.when(sends_part)
    def _():
        for peer in chan_peers:
            part_copy(peer).start()
        part_in[me] = part(core)[...]

    @pl.when(now > 0)
    def _():
        halo.start()

    lag = lax.broadcasted_iota(i32, band.shape, 0) - lax.broadcasted_iota(i32, band.shape, 1)
    band[...] = jnp.where((lag >= 0) & (lag < length), 1.0, 0.0).astype(bf16)

    loads[1].wait()
    loads[2].wait()
    templates, per_template = listed_in.shape
    names = listed_in[...]
    column = lax.broadcasted_iota(i32, names.shape, 1)
    key = jnp.full(names.shape, -1, i32)
    code = (lax.broadcasted_iota(i32, names.shape, 0) * 32 + column) * LANES + moves_in[...]
    counts = jnp.zeros((templates, 1), i32)
    for place, group in ((0, me), (SEL, sibling)):
        from_first = names - group * channels
        inside = (from_first >= 0) & (from_first < channels)
        mine = jnp.where(inside, 1, 0)
        in_row = before(mine, 1)
        full_row = jnp.sum(mine, axis=1, keepdims=True)
        rank = in_row + before(jnp.broadcast_to(full_row, mine.shape), 0)
        key = jnp.where(inside & (rank < SLOTS), rank + place, key)
        code = jnp.where(inside, code + from_first * (1 << 17), code)
        if place == 0:
            counts = full_row
    lane32 = lax.broadcasted_iota(i32, (templates, LANES), 1)
    found = jnp.zeros((templates, LANES), i32)
    for c in range(per_template):
        found = found + jnp.where(
            lane32 == jnp.broadcast_to(key[:, c : c + 1], lane32.shape),
            jnp.broadcast_to(code[:, c : c + 1], lane32.shape), 0,
        )
    ahead = jnp.where(
        lax.broadcasted_iota(i32, lane32.shape, 0) < lane32, jnp.broadcast_to(counts, lane32.shape), 0
    )
    tab_v[0:1, :] = jnp.sum(found, axis=0, keepdims=True)
    tab_v[1:2, :] = jnp.minimum(jnp.sum(ahead, axis=0, keepdims=True), SLOTS)
    to_scalars = pltpu.make_async_copy(tab_v, tab, in_sems.at[4])
    to_scalars.start()

    def lay(ref, first):
        for i in range(ref.shape[1] // LANES):
            for c in range(0, channels, 16):
                flat_rows[pl.ds(c * pitch + first + i, 16, stride=pitch), :] = ref[
                    c : c + 16, i * LANES : (i + 1) * LANES
                ].astype(f32)

    loads[3].wait()
    lay(x_in, 0)
    to_scalars.wait()

    entries = tab_v[0:1, :]
    rows_of = (entries >> 7) & 31
    taken = jnp.where(rows_of // 16 == core, ((entries >> 12) & 31) * 16 + rows_of % 16, -1)
    taken = jnp.broadcast_to(taken, (n_chan * 16, LANES))
    hot = jnp.where(lax.broadcasted_iota(i32, taken.shape, 0) == taken, 1.0, 0.0)
    for b in range(n_chan * 16 // LANES):
        takes[:, b * LANES : (b + 1) * LANES] = hot[b * LANES : (b + 1) * LANES].T.astype(bf16)

    lane = lax.broadcasted_iota(i32, (half_tiles, LANES), 1)
    left = lane < HALF_LANES
    together = 4

    def prepare(group, half):
        squares = []
        first = half * half_tiles
        for u in range(together):
            station = group * together + u
            for d in range(PER):
                entry = tab[0, station * PER + d]
                move = entry & (LANES - 1)
                record = rows[entry >> 17][first : first + half_tiles + 8]
                at = u * PER + d
                turned[at] = pltpu.roll(record, lax.rem(LANES - move, LANES), 1)
                here = lane < LANES - move
                parts = [turned[at, b : b + half_tiles, :] for b in range(BLOCKS + 1)]
                shifted = [jnp.where(here, parts[b], parts[b + 1]) for b in range(BLOCKS)]
                swung = [pltpu.roll(s, HALF_LANES, 1) for s in shifted]
                later = [jnp.where(left, swung[b], swung[b + 1]) for b in range(WAVE_BLOCKS)]
                for phase, tile in enumerate((shifted[:WAVE_BLOCKS], later)):
                    at_row = (at % 2 * 2 + phase) * tiles + first
                    lhs[group * (together * PER // 2) + at // 2, at_row : at_row + half_tiles, :] = jnp.concatenate(
                        [s.astype(bf16) for s in tile], axis=1
                    )
                squares.append(jnp.concatenate([(s * s).astype(bf16) for s in shifted], axis=1))
        energy = jnp.dot(jnp.concatenate(squares, axis=0), band[...], preferred_element_type=f32)
        factor = lax.rsqrt(energy / length + EPS) / math.sqrt(length)
        for u in range(together):
            for d in range(PER):
                at = (u * PER + d) * half_tiles
                scale[group * together + u, d, first : first + half_tiles, :] = factor[at : at + half_tiles]

    each(STATIONS // together, lambda g: prepare(g, 0))

    def chosen_copy(other, d):
        return pltpu.make_async_remote_copy(
            src_ref=chosen.at[other], dst_ref=chosen_in.at[block_of * HALVES + core],
            send_sem=sems.at[4], recv_sem=sems.at[5],
            device_id=(sibling if other else me, row_peer(d)), device_id_type=MESH,
        )

    @pl.when(sends_part)
    def _():
        wait_for(part_in, n_chan - 1, sems.at[3])
        picked = jnp.dot(
            takes[...], part_in[...].reshape(n_chan * 16, LANES), preferred_element_type=f32
        ).astype(bf16)
        for other in (1, 0):
            chosen[other] = picked[other * SEL : (other + 1) * SEL]
        for d in (2, 1, 3, 0):
            for other in (1, 0):
                if other or d:
                    chosen_copy(other, d).start()
        chosen_in[block_of * HALVES + core] = chosen[0]

    @pl.when(now < n_tm - 1)
    def _():
        halo.wait_recv()

    @pl.when(now == n_tm - 1)
    def _():
        halo_in[...] = jnp.zeros_like(halo_in)

    lay(halo_in, tiles)
    each(STATIONS // together, lambda g: prepare(g, 1))

    @pl.when(sends_part)
    def _():
        wait_for(chosen_in, PARTS - 1, sems.at[5])

    @pl.when(jnp.logical_not(sends_part))
    def _():
        wait_for(chosen_in, PARTS, sems.at[5])

    for b in range(WAVE_BLOCKS):
        halves = [chosen_in[b * HALVES + h].astype(f32) for h in range(HALVES)]
        chosen_all[:, b * LANES : (b + 1) * LANES] = halves[0] + halves[1]

    running[0] = jnp.zeros((tiles, LANES), f32)

    at_once = 20
    left_all = lax.broadcasted_iota(i32, (tiles, LANES), 1) < HALF_LANES

    def toeplitz_of(k):
        wide = jnp.broadcast_to(chosen_all[pl.ds(k, 1), :], (HALF_LANES, WAVE_BLOCKS * LANES))
        return pltpu.roll(wide, 0, 1, stride=1, stride_axis=0).astype(bf16)

    def correlate(group, total):
        numers = []
        for p in range(at_once * PER // 2):
            pair = group * (at_once * PER // 2) + p
            both = lax.dot_general(
                lhs[pair], jnp.concatenate([toeplitz_of(pair * 2), toeplitz_of(pair * 2 + 1)], axis=0),
                (((1,), (1,)), ((), ())), preferred_element_type=f32,
            )
            first, second, third, fourth = (both[i * tiles : (i + 1) * tiles] for i in range(4))
            swapped = pltpu.roll(jnp.where(left_all, second, third), HALF_LANES, 1)
            numers.append(jnp.where(left_all, first, swapped))
            numers.append(jnp.where(left_all, swapped, fourth))
        for u in range(at_once):
            station = group * at_once + u
            for d in range(PER):
                total = total + numers[u * PER + d] * scale[station, d]
            running[station + 1] = total
        return total

    lax.fori_loop(0, STATIONS // at_once, correlate, jnp.zeros((tiles, LANES), f32))

    def summed(template):
        return running[tab[1, template + 1] // PER] - running[tab[1, template] // PER]

    places = far_chips + [chip]
    share = len(places) // PAIR_PIECES

    def pair_copy(piece):
        span = pl.ds(piece * share, share)
        return pltpu.make_async_remote_copy(
            src_ref=pair_out.at[span], dst_ref=pair_in.at[span],
            send_sem=pair_sems.at[0, piece], recv_sem=pair_sems.at[1, piece],
            device_id=(sibling, now), device_id_type=MESH,
        )

    for piece in range(PAIR_PIECES):
        for i in range(piece * share, (piece + 1) * share):
            pair_out[i] = summed(places[i] * HALVES + 1 - core)
        pair_copy(piece).start()

    def stack_copy(place):
        return pltpu.make_async_remote_copy(
            src_ref=outgoing.at[place], dst_ref=incoming.at[chip],
            send_sem=sems.at[6], recv_sem=sems.at[7],
            device_id=(place * HALVES + core, now), device_id_type=MESH,
        )

    for i, place in enumerate(places):
        mine_out[i] = summed(place * HALVES + core)
    stack = jnp.zeros((tiles, LANES), f32)
    for i, place in enumerate(places):
        if i % share == 0:
            pair_copy(i // share).wait_recv()
        stack = mine_out[i] + pair_in[i]
        if i < len(far_chips):
            outgoing[place] = stack.astype(bf16)
            stack_copy(place).start()
    if far_chips:
        wait_for(incoming, len(far_chips), sems.at[7])
    for place in far_chips:
        stack = stack + incoming[place].astype(f32)
    stack_out[...] = stack
    peak_mine[...] = jnp.max(jnp.abs(stack).reshape(tiles // 8, 8, LANES), axis=0)

    def peak_copy(i):
        return pltpu.make_async_remote_copy(
            src_ref=peak_mine, dst_ref=peak_in.at[now],
            send_sem=sems.at[8], recv_sem=sems.at[9],
            device_id=(me, tm_peer(i + 1)), device_id_type=MESH,
        )

    for i in range(n_tm - 1):
        peak_copy(i).start()
    wait_for(peak_in, n_tm - 1, sems.at[9])
    peak = peak_mine[...]
    for i in range(n_tm - 1):
        peak = jnp.maximum(peak, peak_in[tm_peer(i + 1)])
    peak_out[...] = peak

    @pl.when(now > 0)
    def _():
        halo.wait_send()

    @pl.when(sends_part)
    def _():
        wait_for(part_in, n_chan - 1, sems.at[2])
        wait_for(chosen_in, 2 * ROW - 1, sems.at[4])

    for piece in range(PAIR_PIECES):
        pair_copy(piece).wait_send()
    if far_chips:
        wait_for(outgoing, len(far_chips), sems.at[6])
    wait_for(peak_in, n_tm - 1, sems.at[8])


def on_device(n_chan, n_tm, seismic, waveforms, channel_list, moveouts):
    channels, piece = seismic.shape
    length = waveforms.shape[2]
    tiles = piece // LANES
    pitch = tiles + 8
    f32, bf16, i32 = jnp.float32, jnp.bfloat16, jnp.int32
    stack, peak = pl.pallas_call(
        functools.partial(kernel, n_chan, n_tm, length, channels),
        out_shape=(
            jax.ShapeDtypeStruct((tiles, LANES), f32),
            jax.ShapeDtypeStruct((8, LANES), f32),
        ),
        in_specs=[pl.BlockSpec(memory_space=pltpu.HBM)] * 4,
        out_specs=[pl.BlockSpec(memory_space=pltpu.VMEM)] * 2,
        scratch_shapes=[
            pltpu.VMEM(channel_list.shape, i32),
            pltpu.VMEM(moveouts.shape, i32),
            pltpu.VMEM((waveforms.shape[1], 1, length), f32),
            pltpu.VMEM((channels, piece), bf16),
            pltpu.VMEM((channels, HALO * LANES), bf16),
            pltpu.VMEM((8, LANES), i32),
            pltpu.SMEM((8, LANES), i32),
            pltpu.VMEM((channels, pitch, LANES), f32),
            pltpu.VMEM((4 * PER, tiles // 2 + 8, LANES), f32),
            pltpu.VMEM((SLOTS // 2, 4 * tiles, WAVE_BLOCKS * LANES), bf16),
            pltpu.VMEM((STATIONS, PER, tiles, LANES), f32),
            pltpu.VMEM((BLOCKS * LANES, LANES), bf16),
            pltpu.VMEM((32, WAVE_BLOCKS * LANES), bf16),
            pltpu.VMEM((n_chan, 16, LANES), bf16),
            pltpu.VMEM((2 * SEL, n_chan * 16), bf16),
            pltpu.VMEM((2, SEL, LANES), bf16),
            pltpu.VMEM((2 * ROW, SEL, LANES), bf16),
            pltpu.VMEM((SEL, WAVE_BLOCKS * LANES), f32),
            pltpu.VMEM((STATIONS + 1, tiles, LANES), f32),
            pltpu.VMEM((n_chan // HALVES, tiles, LANES), f32),
            pltpu.VMEM((n_chan // HALVES, tiles, LANES), f32),
            pltpu.VMEM((n_chan // HALVES, tiles, LANES), f32),
            pltpu.VMEM((n_chan // HALVES, tiles, LANES), bf16),
            pltpu.VMEM((n_chan // HALVES, tiles, LANES), bf16),
            pltpu.VMEM((8, LANES), f32),
            pltpu.VMEM((n_tm, 8, LANES), f32),
            pltpu.SemaphoreType.DMA((10,)),
            pltpu.SemaphoreType.DMA((2, PAIR_PIECES)),
            pltpu.SemaphoreType.DMA((5,)),
        ],
        compiler_params=pltpu.CompilerParams(
            collective_id=0, has_side_effects=True, vmem_limit_bytes=GRANT
        ),
    )(channel_list, moveouts, seismic, jnp.transpose(waveforms, (1, 0, 2)))
    return stack.reshape(1, piece), jnp.max(peak).reshape(1)


def solution(mesh):
    return jax.shard_map(
        functools.partial(on_device, mesh.shape["chan"], mesh.shape["tm"]),
        mesh=mesh,
        in_specs=(P("chan", "tm"), P("chan", None, None), P(), P()),
        out_specs=(P("chan", "tm"), P("chan")),
        check_vma=False,
    )
```

```python
import functools
import math

import jax
import jax.numpy as jnp
from jax import lax
from jax.experimental import pallas as pl
from jax.experimental.pallas import tpu as pltpu
from jax.sharding import PartitionSpec as P

LANES = 128
HALF_LANES = 64
STATIONS = 20
PER = 3
SLOTS = STATIONS * PER
SEL = 64
HALO = 4
BLOCKS = 4
WAVE_BLOCKS = 3
HALVES = 2
PARTS = WAVE_BLOCKS * HALVES
ROW = 4
RING = 8
PAIR_PIECES = 2
DIRECT = 1
EPS = 1e-05
GRANT = 55200 * 1024
MESH = pl.DeviceIdType.MESH


def each(count, body, unroll=1):
    def step(i, carry):
        for u in range(unroll):
            body(i * unroll + u)
        return carry

    assert count % unroll == 0
    lax.fori_loop(0, count // unroll, step, 0)


def ring_offsets(n_chan):
    chips = n_chan // HALVES
    depth = min(RING, chips)
    offsets = [(dy, dz) for dy in range(chips // depth) for dz in range(depth)]
    return sorted(offsets, key=lambda o: (-(o[0] + min(o[1], depth - o[1])), o))


def before(x, axis):
    index = lax.broadcasted_iota(jnp.int32, x.shape, axis)
    step, total = 1, x
    while step < 32:
        total = total + jnp.where(index >= step, pltpu.roll(total, step, axis), 0)
        step *= 2
    return total - x


def kernel(
    n_chan, n_tm, length, channels,
    listed, moves, seis, waves,
    stack_out, peak_out,
    listed_in, moves_in, waves_in, x_in, halo_in, tab_v, tab,
    rows, turned, lhs, scale, band,
    normed, part_in, takes, chosen, chosen_in, chosen_all,
    running, mine_out, pair_out, pair_in, outgoing, incoming, peak_mine, peak_in,
    sems, pair_sems, in_sems,
):
    me = lax.axis_index("chan")
    now = lax.axis_index("tm")
    core = lax.rem(me, HALVES)
    across = lax.rem(now, ROW)
    row_start = now - across
    sibling = me + 1 - 2 * core
    tiles = stack_out.shape[0]
    pitch = rows.shape[1]
    flat_rows = rows.reshape(channels * pitch, LANES)
    half_tiles = tiles // 2
    f32, bf16, i32 = jnp.float32, jnp.bfloat16, jnp.int32

    def wait_for(ref, blocks, sem):
        span = ref.at[pl.ds(0, blocks)]
        pltpu.make_async_copy(span, span, sem).wait()

    chip = me // HALVES
    depth = min(RING, n_chan // HALVES)
    offsets = ring_offsets(n_chan)

    def chip_at(offset):
        dy, dz = offset
        y, z = chip // depth, lax.rem(chip, depth)
        return lax.rem(y + dy, n_chan // HALVES // depth) * depth + lax.rem(z + dz, depth)

    chan_peers = [
        chip_at(offset) * HALVES + lax.rem(core + dc, HALVES)
        for offset in offsets for dc in range(HALVES) if offset != (0, 0) or dc
    ]
    far_chips = [chip_at(offset) for offset in offsets if offset != (0, 0)]

    def tm_peer(d):
        return lax.rem(now + d, n_tm)

    def row_peer(d):
        return row_start + lax.rem(across + d, ROW)

    barrier = pltpu.get_barrier_semaphore()

    loads = [
        pltpu.make_async_copy(src, dst, in_sems.at[i])
        for i, (src, dst) in enumerate(
            ((waves, waves_in), (listed, listed_in), (moves, moves_in), (seis, x_in))
        )
    ]
    loads[0].start()

    def greet(group, piece):
        pl.semaphore_signal(barrier, inc=1, device_id=(group, piece), device_id_type=MESH)

    for peer in chan_peers[: n_chan // 2]:
        greet(peer, now)
    for i in range(n_tm - 1):
        greet(me, tm_peer(i + 1))
    for i in range(ROW - 1):
        greet(sibling, row_peer(i + 1))
    for peer in chan_peers[n_chan // 2 :]:
        greet(peer, now)

    for copy in loads[1:]:
        copy.start()

    loads[0].wait()
    w = waves_in[:, 0, :]
    centered = w - jnp.mean(w, axis=-1, keepdims=True)
    factor = lax.rsqrt(jnp.mean(centered * centered, axis=-1, keepdims=True) + EPS) / math.sqrt(length)
    normed[...] = jnp.zeros_like(normed)
    normed[0 : w.shape[0], 0:length] = (centered * factor).astype(bf16)

    pl.semaphore_wait(barrier, n_chan - 1 + n_tm - 1 + ROW - 1)

    halo = pltpu.make_async_remote_copy(
        src_ref=seis.at[:, pl.ds(0, HALO * LANES)], dst_ref=halo_in,
        send_sem=sems.at[0], recv_sem=sems.at[1],
        device_id=(me, jnp.maximum(now - 1, 0)), device_id_type=MESH,
    )

    sends_part = across < WAVE_BLOCKS
    block_of = jnp.minimum(across, WAVE_BLOCKS - 1)

    def part(half):
        return normed.at[pl.ds(half * 16, 16), pl.ds(block_of * LANES, LANES)]

    def part_copy(peer):
        return pltpu.make_async_remote_copy(
            src_ref=part(lax.rem(peer, HALVES)), dst_ref=part_in.at[me],
            send_sem=sems.at[2], recv_sem=sems.at[3],
            device_id=(peer, now), device_id_type=MESH,
        )

    @pl.when(sends_part)
    def _():
        for peer in chan_peers:
            part_copy(peer).start()
        part_in[me] = part(core)[...]

    @pl.when(now > 0)
    def _():
        halo.start()

    lag = lax.broadcasted_iota(i32, band.shape, 0) - lax.broadcasted_iota(i32, band.shape, 1)
    band[...] = jnp.where((lag >= 0) & (lag < length), 1.0, 0.0).astype(bf16)

    loads[1].wait()
    loads[2].wait()
    templates, per_template = listed_in.shape
    names = listed_in[...]
    column = lax.broadcasted_iota(i32, names.shape, 1)
    key = jnp.full(names.shape, -1, i32)
    code = (lax.broadcasted_iota(i32, names.shape, 0) * 32 + column) * LANES + moves_in[...]
    counts = jnp.zeros((templates, 1), i32)
    for place, group in ((0, me), (SEL, sibling)):
        from_first = names - group * channels
        inside = (from_first >= 0) & (from_first < channels)
        mine = jnp.where(inside, 1, 0)
        in_row = before(mine, 1)
        full_row = jnp.sum(mine, axis=1, keepdims=True)
        rank = in_row + before(jnp.broadcast_to(full_row, mine.shape), 0)
        key = jnp.where(inside & (rank < SLOTS), rank + place, key)
        code = jnp.where(inside, code + from_first * (1 << 17), code)
        if place == 0:
            counts = full_row
    lane32 = lax.broadcasted_iota(i32, (templates, LANES), 1)
    found = jnp.zeros((templates, LANES), i32)
    for c in range(per_template):
        found = found + jnp.where(
            lane32 == jnp.broadcast_to(key[:, c : c + 1], lane32.shape),
            jnp.broadcast_to(code[:, c : c + 1], lane32.shape), 0,
        )
    ahead = jnp.where(
        lax.broadcasted_iota(i32, lane32.shape, 0) < lane32, jnp.broadcast_to(counts, lane32.shape), 0
    )
    tab_v[0:1, :] = jnp.sum(found, axis=0, keepdims=True)
    tab_v[1:2, :] = jnp.minimum(jnp.sum(ahead, axis=0, keepdims=True), SLOTS)
    to_scalars = pltpu.make_async_copy(tab_v, tab, in_sems.at[4])
    to_scalars.start()

    def lay(ref, first):
        for i in range(ref.shape[1] // LANES):
            for c in range(0, channels, 16):
                flat_rows[pl.ds(c * pitch + first + i, 16, stride=pitch), :] = ref[
                    c : c + 16, i * LANES : (i + 1) * LANES
                ].astype(f32)

    loads[3].wait()
    lay(x_in, 0)
    to_scalars.wait()

    entries = tab_v[0:1, :]
    rows_of = (entries >> 7) & 31
    taken = jnp.where(rows_of // 16 == core, ((entries >> 12) & 31) * 16 + rows_of % 16, -1)
    taken = jnp.broadcast_to(taken, (n_chan * 16, LANES))
    hot = jnp.where(lax.broadcasted_iota(i32, taken.shape, 0) == taken, 1.0, 0.0)
    for b in range(n_chan * 16 // LANES):
        takes[:, b * LANES : (b + 1) * LANES] = hot[b * LANES : (b + 1) * LANES].T.astype(bf16)

    lane = lax.broadcasted_iota(i32, (half_tiles, LANES), 1)
    left = lane < HALF_LANES
    together = 4

    def prepare(group, half):
        squares = []
        first = half * half_tiles
        for u in range(together):
            station = group * together + u
            for d in range(PER):
                entry = tab[0, station * PER + d]
                move = entry & (LANES - 1)
                record = rows[entry >> 17][first : first + half_tiles + 8]
                at = u * PER + d
                turned[at] = pltpu.roll(record, lax.rem(LANES - move, LANES), 1)
                here = lane < LANES - move
                parts = [turned[at, b : b + half_tiles, :] for b in range(BLOCKS + 1)]
                shifted = [jnp.where(here, parts[b], parts[b + 1]) for b in range(BLOCKS)]
                swung = [pltpu.roll(s, HALF_LANES, 1) for s in shifted]
                later = [jnp.where(left, swung[b], swung[b + 1]) for b in range(WAVE_BLOCKS)]
                for phase, tile in enumerate((shifted[:WAVE_BLOCKS], later)):
                    at_row = (at % 2 * 2 + phase) * tiles + first
                    lhs[group * (together * PER // 2) + at // 2, at_row : at_row + half_tiles, :] = jnp.concatenate(
                        [s.astype(bf16) for s in tile], axis=1
                    )
                squares.append(jnp.concatenate([(s * s).astype(bf16) for s in shifted], axis=1))
        energy = jnp.dot(jnp.concatenate(squares, axis=0), band[...], preferred_element_type=f32)
        factor = lax.rsqrt(energy / length + EPS) / math.sqrt(length)
        for u in range(together):
            for d in range(PER):
                at = (u * PER + d) * half_tiles
                scale[group * together + u, d, first : first + half_tiles, :] = factor[at : at + half_tiles]

    each(STATIONS // together, lambda g: prepare(g, 0))

    def chosen_copy(other, d):
        return pltpu.make_async_remote_copy(
            src_ref=chosen.at[other], dst_ref=chosen_in.at[block_of * HALVES + core],
            send_sem=sems.at[4], recv_sem=sems.at[5],
            device_id=(sibling if other else me, row_peer(d)), device_id_type=MESH,
        )

    @pl.when(sends_part)
    def _():
        wait_for(part_in, n_chan - 1, sems.at[3])
        picked = jnp.dot(
            takes[...], part_in[...].reshape(n_chan * 16, LANES), preferred_element_type=f32
        ).astype(bf16)
        for other in (1, 0):
            chosen[other] = picked[other * SEL : (other + 1) * SEL]
        for d in (2, 1, 3, 0):
            for other in (1, 0):
                if other or d:
                    chosen_copy(other, d).start()
        chosen_in[block_of * HALVES + core] = chosen[0]

    @pl.when(now < n_tm - 1)
    def _():
        halo.wait_recv()

    @pl.when(now == n_tm - 1)
    def _():
        halo_in[...] = jnp.zeros_like(halo_in)

    lay(halo_in, tiles)
    each(STATIONS // together, lambda g: prepare(g, 1))

    @pl.when(sends_part)
    def _():
        wait_for(chosen_in, PARTS - 1, sems.at[5])

    @pl.when(jnp.logical_not(sends_part))
    def _():
        wait_for(chosen_in, PARTS, sems.at[5])

    for b in range(WAVE_BLOCKS):
        halves = [chosen_in[b * HALVES + h].astype(f32) for h in range(HALVES)]
        chosen_all[:, b * LANES : (b + 1) * LANES] = halves[0] + halves[1]

    running[0] = jnp.zeros((tiles, LANES), f32)

    at_once = 20
    left_all = lax.broadcasted_iota(i32, (tiles, LANES), 1) < HALF_LANES

    def toeplitz_of(k):
        wide = jnp.broadcast_to(chosen_all[pl.ds(k, 1), :], (HALF_LANES, WAVE_BLOCKS * LANES))
        return pltpu.roll(wide, 0, 1, stride=1, stride_axis=0).astype(bf16)

    def correlate(group, total):
        numers = []
        for p in range(at_once * PER // 2):
            pair = group * (at_once * PER // 2) + p
            both = lax.dot_general(
                lhs[pair], jnp.concatenate([toeplitz_of(pair * 2), toeplitz_of(pair * 2 + 1)], axis=0),
                (((1,), (1,)), ((), ())), preferred_element_type=f32,
            )
            first, second, third, fourth = (both[i * tiles : (i + 1) * tiles] for i in range(4))
            swapped = pltpu.roll(jnp.where(left_all, second, third), HALF_LANES, 1)
            numers.append(jnp.where(left_all, first, swapped))
            numers.append(jnp.where(left_all, swapped, fourth))
        for u in range(at_once):
            station = group * at_once + u
            for d in range(PER):
                total = total + numers[u * PER + d] * scale[station, d]
            running[station + 1] = total
        return total

    lax.fori_loop(0, STATIONS // at_once, correlate, jnp.zeros((tiles, LANES), f32))

    def summed(template):
        return running[tab[1, template + 1] // PER] - running[tab[1, template] // PER]

    def stack_copy(peer):
        return pltpu.make_async_remote_copy(
            src_ref=outgoing.at[peer], dst_ref=incoming.at[me],
            send_sem=sems.at[6], recv_sem=sems.at[7],
            device_id=(peer, now), device_id_type=MESH,
        )

    def send_stack(peer, total):
        outgoing[peer] = total.astype(bf16)
        stack_copy(peer).start()

    direct = far_chips[:DIRECT]
    for place in direct:
        for c in range(HALVES):
            send_stack(place * HALVES + c, summed(place * HALVES + c))

    places = far_chips[len(direct) :] + [chip]
    cuts = [0, (len(places) + 1) // 2, len(places)]

    def pair_copy(piece):
        span = pl.ds(cuts[piece], cuts[piece + 1] - cuts[piece])
        return pltpu.make_async_remote_copy(
            src_ref=pair_out.at[span], dst_ref=pair_in.at[span],
            send_sem=pair_sems.at[0, piece], recv_sem=pair_sems.at[1, piece],
            device_id=(sibling, now), device_id_type=MESH,
        )

    for piece in range(PAIR_PIECES):
        for i in range(cuts[piece], cuts[piece + 1]):
            pair_out[i] = summed(places[i] * HALVES + 1 - core)
        pair_copy(piece).start()
    for i, place in enumerate(places):
        mine_out[i] = summed(place * HALVES + core)
    stack = jnp.zeros((tiles, LANES), f32)
    for i, place in enumerate(places):
        if i in cuts:
            pair_copy(cuts.index(i)).wait_recv()
        stack = mine_out[i] + pair_in[i]
        if i < len(places) - 1:
            send_stack(place * HALVES + core, stack)
    received = [place * HALVES + c for place in direct for c in range(HALVES)]
    received += [place * HALVES + core for place in places[:-1]]
    wait_for(incoming, len(received), sems.at[7])
    for peer in received:
        stack = stack + incoming[peer].astype(f32)
    stack_out[...] = stack
    peak_mine[...] = jnp.max(jnp.abs(stack).reshape(tiles // 8, 8, LANES), axis=0)

    def peak_copy(i):
        return pltpu.make_async_remote_copy(
            src_ref=peak_mine, dst_ref=peak_in.at[now],
            send_sem=sems.at[8], recv_sem=sems.at[9],
            device_id=(me, tm_peer(i + 1)), device_id_type=MESH,
        )

    for i in range(n_tm - 1):
        peak_copy(i).start()
    wait_for(peak_in, n_tm - 1, sems.at[9])
    peak = peak_mine[...]
    for i in range(n_tm - 1):
        peak = jnp.maximum(peak, peak_in[tm_peer(i + 1)])
    peak_out[...] = peak

    @pl.when(now > 0)
    def _():
        halo.wait_send()

    @pl.when(sends_part)
    def _():
        wait_for(part_in, n_chan - 1, sems.at[2])
        wait_for(chosen_in, 2 * ROW - 1, sems.at[4])

    for piece in range(PAIR_PIECES):
        pair_copy(piece).wait_send()
    wait_for(outgoing, len(received), sems.at[6])
    wait_for(peak_in, n_tm - 1, sems.at[8])


def on_device(n_chan, n_tm, seismic, waveforms, channel_list, moveouts):
    channels, piece = seismic.shape
    length = waveforms.shape[2]
    tiles = piece // LANES
    pitch = tiles + 8
    f32, bf16, i32 = jnp.float32, jnp.bfloat16, jnp.int32
    stack, peak = pl.pallas_call(
        functools.partial(kernel, n_chan, n_tm, length, channels),
        out_shape=(
            jax.ShapeDtypeStruct((tiles, LANES), f32),
            jax.ShapeDtypeStruct((8, LANES), f32),
        ),
        in_specs=[pl.BlockSpec(memory_space=pltpu.HBM)] * 4,
        out_specs=[pl.BlockSpec(memory_space=pltpu.VMEM)] * 2,
        scratch_shapes=[
            pltpu.VMEM(channel_list.shape, i32),
            pltpu.VMEM(moveouts.shape, i32),
            pltpu.VMEM((waveforms.shape[1], 1, length), f32),
            pltpu.VMEM((channels, piece), bf16),
            pltpu.VMEM((channels, HALO * LANES), bf16),
            pltpu.VMEM((8, LANES), i32),
            pltpu.SMEM((8, LANES), i32),
            pltpu.VMEM((channels, pitch, LANES), f32),
            pltpu.VMEM((4 * PER, tiles // 2 + 8, LANES), f32),
            pltpu.VMEM((SLOTS // 2, 4 * tiles, WAVE_BLOCKS * LANES), bf16),
            pltpu.VMEM((STATIONS, PER, tiles, LANES), f32),
            pltpu.VMEM((BLOCKS * LANES, LANES), bf16),
            pltpu.VMEM((32, WAVE_BLOCKS * LANES), bf16),
            pltpu.VMEM((n_chan, 16, LANES), bf16),
            pltpu.VMEM((2 * SEL, n_chan * 16), bf16),
            pltpu.VMEM((2, SEL, LANES), bf16),
            pltpu.VMEM((2 * ROW, SEL, LANES), bf16),
            pltpu.VMEM((SEL, WAVE_BLOCKS * LANES), f32),
            pltpu.VMEM((STATIONS + 1, tiles, LANES), f32),
            pltpu.VMEM((n_chan // HALVES, tiles, LANES), f32),
            pltpu.VMEM((n_chan // HALVES, tiles, LANES), f32),
            pltpu.VMEM((n_chan // HALVES, tiles, LANES), f32),
            pltpu.VMEM((n_chan, tiles, LANES), bf16),
            pltpu.VMEM((n_chan, tiles, LANES), bf16),
            pltpu.VMEM((8, LANES), f32),
            pltpu.VMEM((n_tm, 8, LANES), f32),
            pltpu.SemaphoreType.DMA((10,)),
            pltpu.SemaphoreType.DMA((2, PAIR_PIECES)),
            pltpu.SemaphoreType.DMA((5,)),
        ],
        compiler_params=pltpu.CompilerParams(
            collective_id=0, has_side_effects=True, vmem_limit_bytes=GRANT
        ),
    )(channel_list, moveouts, seismic, jnp.transpose(waveforms, (1, 0, 2)))
    return stack.reshape(1, piece), jnp.max(peak).reshape(1)


def solution(mesh):
    return jax.shard_map(
        functools.partial(on_device, mesh.shape["chan"], mesh.shape["tm"]),
        mesh=mesh,
        in_specs=(P("chan", "tm"), P("chan", None, None), P(), P()),
        out_specs=(P("chan", "tm"), P("chan")),
        check_vma=False,
    )
```

```python
import functools
import math

import jax
import jax.numpy as jnp
from jax import lax
from jax.experimental import pallas as pl
from jax.experimental.pallas import tpu as pltpu
from jax.sharding import PartitionSpec as P

LANES = 128
HALF_LANES = 64
STATIONS = 20
PER = 3
SLOTS = STATIONS * PER
SEL = 64
HALO = 4
BLOCKS = 4
WAVE_BLOCKS = 3
HALVES = 2
PARTS = WAVE_BLOCKS * HALVES
ROW = 4
RING = 8
PAIR_PIECES = 2
EPS = 1e-05
GRANT = 55200 * 1024
MESH = pl.DeviceIdType.MESH


def each(count, body, unroll=1):
    def step(i, carry):
        for u in range(unroll):
            body(i * unroll + u)
        return carry

    assert count % unroll == 0
    lax.fori_loop(0, count // unroll, step, 0)


def ring_offsets(n_chan):
    chips = n_chan // HALVES
    depth = min(RING, chips)
    offsets = [(dy, dz) for dy in range(chips // depth) for dz in range(depth)]
    return sorted(offsets, key=lambda o: (-(o[0] + min(o[1], depth - o[1])), o))


def before(x, axis):
    index = lax.broadcasted_iota(jnp.int32, x.shape, axis)
    step, total = 1, x
    while step < 32:
        total = total + jnp.where(index >= step, pltpu.roll(total, step, axis), 0)
        step *= 2
    return total - x


def kernel(
    n_chan, n_tm, length, channels,
    listed, moves, seis, waves,
    stack_out, peak_out,
    listed_in, moves_in, waves_in, x_in, halo_in, tab_v, tab,
    rows, turned, lhs, scale, band,
    normed, part_in, takes, chosen, chosen_in, chosen_all,
    running, mine_out, pair_out, pair_in, outgoing, incoming, peak_mine, peak_in,
    sems, pair_sems, in_sems,
):
    me = lax.axis_index("chan")
    now = lax.axis_index("tm")
    core = lax.rem(me, HALVES)
    across = lax.rem(now, ROW)
    row_start = now - across
    sibling = me + 1 - 2 * core
    tiles = stack_out.shape[0]
    pitch = rows.shape[1]
    flat_rows = rows.reshape(channels * pitch, LANES)
    half_tiles = tiles // 2
    f32, bf16, i32 = jnp.float32, jnp.bfloat16, jnp.int32

    def wait_for(ref, blocks, sem):
        span = ref.at[pl.ds(0, blocks)]
        pltpu.make_async_copy(span, span, sem).wait()

    chip = me // HALVES
    depth = min(RING, n_chan // HALVES)
    offsets = ring_offsets(n_chan)

    def chip_at(offset):
        dy, dz = offset
        y, z = chip // depth, lax.rem(chip, depth)
        return lax.rem(y + dy, n_chan // HALVES // depth) * depth + lax.rem(z + dz, depth)

    chan_peers = [
        chip_at(offset) * HALVES + lax.rem(core + dc, HALVES)
        for offset in offsets for dc in range(HALVES) if offset != (0, 0) or dc
    ]
    far_chips = [chip_at(offset) for offset in offsets if offset != (0, 0)]

    def tm_peer(d):
        return lax.rem(now + d, n_tm)

    def row_peer(d):
        return row_start + lax.rem(across + d, ROW)

    barrier = pltpu.get_barrier_semaphore()

    loads = [
        pltpu.make_async_copy(src, dst, in_sems.at[i])
        for i, (src, dst) in enumerate(
            ((waves, waves_in), (listed, listed_in), (moves, moves_in), (seis, x_in))
        )
    ]
    loads[0].start()

    def greet(group, piece):
        pl.semaphore_signal(barrier, inc=1, device_id=(group, piece), device_id_type=MESH)

    for peer in chan_peers[: n_chan // 2]:
        greet(peer, now)
    for i in range(n_tm - 1):
        greet(me, tm_peer(i + 1))
    for i in range(ROW - 1):
        greet(sibling, row_peer(i + 1))
    for peer in chan_peers[n_chan // 2 :]:
        greet(peer, now)

    for copy in loads[1:]:
        copy.start()

    loads[0].wait()
    w = waves_in[:, 0, :]
    centered = w - jnp.mean(w, axis=-1, keepdims=True)
    factor = lax.rsqrt(jnp.mean(centered * centered, axis=-1, keepdims=True) + EPS) / math.sqrt(length)
    normed[...] = jnp.zeros_like(normed)
    normed[0 : w.shape[0], 0:length] = (centered * factor).astype(bf16)

    pl.semaphore_wait(barrier, n_chan - 1 + n_tm - 1 + ROW - 1)

    halo = pltpu.make_async_remote_copy(
        src_ref=seis.at[:, pl.ds(0, HALO * LANES)], dst_ref=halo_in,
        send_sem=sems.at[0], recv_sem=sems.at[1],
        device_id=(me, jnp.maximum(now - 1, 0)), device_id_type=MESH,
    )

    sends_part = across < WAVE_BLOCKS
    block_of = jnp.minimum(across, WAVE_BLOCKS - 1)

    def part(half):
        return normed.at[pl.ds(half * 16, 16), pl.ds(block_of * LANES, LANES)]

    def part_copy(peer):
        return pltpu.make_async_remote_copy(
            src_ref=part(lax.rem(peer, HALVES)), dst_ref=part_in.at[me],
            send_sem=sems.at[2], recv_sem=sems.at[3],
            device_id=(peer, now), device_id_type=MESH,
        )

    @pl.when(sends_part)
    def _():
        for peer in chan_peers:
            part_copy(peer).start()
        part_in[me] = part(core)[...]

    @pl.when(now > 0)
    def _():
        halo.start()

    lag = lax.broadcasted_iota(i32, band.shape, 0) - lax.broadcasted_iota(i32, band.shape, 1)
    band[...] = jnp.where((lag >= 0) & (lag < length), 1.0, 0.0).astype(bf16)

    loads[1].wait()
    loads[2].wait()
    templates, per_template = listed_in.shape
    names = listed_in[...]
    column = lax.broadcasted_iota(i32, names.shape, 1)
    key = jnp.full(names.shape, -1, i32)
    code = (lax.broadcasted_iota(i32, names.shape, 0) * 32 + column) * LANES + moves_in[...]
    counts = jnp.zeros((templates, 1), i32)
    for place, group in ((0, me), (SEL, sibling)):
        from_first = names - group * channels
        inside = (from_first >= 0) & (from_first < channels)
        mine = jnp.where(inside, 1, 0)
        in_row = before(mine, 1)
        full_row = jnp.sum(mine, axis=1, keepdims=True)
        rank = in_row + before(jnp.broadcast_to(full_row, mine.shape), 0)
        key = jnp.where(inside & (rank < SLOTS), rank + place, key)
        code = jnp.where(inside, code + from_first * (1 << 17), code)
        if place == 0:
            counts = full_row
    lane32 = lax.broadcasted_iota(i32, (templates, LANES), 1)
    found = jnp.zeros((templates, LANES), i32)
    for c in range(per_template):
        found = found + jnp.where(
            lane32 == jnp.broadcast_to(key[:, c : c + 1], lane32.shape),
            jnp.broadcast_to(code[:, c : c + 1], lane32.shape), 0,
        )
    ahead = jnp.where(
        lax.broadcasted_iota(i32, lane32.shape, 0) < lane32, jnp.broadcast_to(counts, lane32.shape), 0
    )
    tab_v[0:1, :] = jnp.sum(found, axis=0, keepdims=True)
    tab_v[1:2, :] = jnp.minimum(jnp.sum(ahead, axis=0, keepdims=True), SLOTS)
    to_scalars = pltpu.make_async_copy(tab_v, tab, in_sems.at[4])
    to_scalars.start()

    def lay(ref, first):
        for i in range(ref.shape[1] // LANES):
            for c in range(0, channels, 16):
                flat_rows[pl.ds(c * pitch + first + i, 16, stride=pitch), :] = ref[
                    c : c + 16, i * LANES : (i + 1) * LANES
                ].astype(f32)

    loads[3].wait()
    lay(x_in, 0)
    to_scalars.wait()

    entries = tab_v[0:1, :]
    rows_of = (entries >> 7) & 31
    taken = jnp.where(rows_of // 16 == core, ((entries >> 12) & 31) * 16 + rows_of % 16, -1)
    taken = jnp.broadcast_to(taken, (n_chan * 16, LANES))
    hot = jnp.where(lax.broadcasted_iota(i32, taken.shape, 0) == taken, 1.0, 0.0)
    for b in range(n_chan * 16 // LANES):
        takes[:, b * LANES : (b + 1) * LANES] = hot[b * LANES : (b + 1) * LANES].T.astype(bf16)

    lane = lax.broadcasted_iota(i32, (half_tiles, LANES), 1)
    left = lane < HALF_LANES
    together = 4

    def prepare(group, half):
        squares = []
        first = half * half_tiles
        for u in range(together):
            station = group * together + u
            for d in range(PER):
                entry = tab[0, station * PER + d]
                move = entry & (LANES - 1)
                record = rows[entry >> 17][first : first + half_tiles + 8]
                at = u * PER + d
                turned[at] = pltpu.roll(record, lax.rem(LANES - move, LANES), 1)
                here = lane < LANES - move
                parts = [turned[at, b : b + half_tiles, :] for b in range(BLOCKS + 1)]
                shifted = [jnp.where(here, parts[b], parts[b + 1]) for b in range(BLOCKS)]
                swung = [pltpu.roll(s, HALF_LANES, 1) for s in shifted]
                later = [jnp.where(left, swung[b], swung[b + 1]) for b in range(WAVE_BLOCKS)]
                for phase, tile in enumerate((shifted[:WAVE_BLOCKS], later)):
                    at_row = (at % 2 * 2 + phase) * tiles + first
                    lhs[group * (together * PER // 2) + at // 2, at_row : at_row + half_tiles, :] = jnp.concatenate(
                        [s.astype(bf16) for s in tile], axis=1
                    )
                squares.append(jnp.concatenate([(s * s).astype(bf16) for s in shifted], axis=1))
        energy = jnp.dot(jnp.concatenate(squares, axis=0), band[...], preferred_element_type=f32)
        factor = lax.rsqrt(energy / length + EPS) / math.sqrt(length)
        for u in range(together):
            for d in range(PER):
                at = (u * PER + d) * half_tiles
                scale[group * together + u, d, first : first + half_tiles, :] = factor[at : at + half_tiles]

    each(STATIONS // together, lambda g: prepare(g, 0))

    def chosen_copy(other, d):
        return pltpu.make_async_remote_copy(
            src_ref=chosen.at[other], dst_ref=chosen_in.at[block_of * HALVES + core],
            send_sem=sems.at[4], recv_sem=sems.at[5],
            device_id=(sibling if other else me, row_peer(d)), device_id_type=MESH,
        )

    @pl.when(sends_part)
    def _():
        wait_for(part_in, n_chan - 1, sems.at[3])
        picked = jnp.dot(
            takes[...], part_in[...].reshape(n_chan * 16, LANES), preferred_element_type=f32
        ).astype(bf16)
        for other in (1, 0):
            chosen[other] = picked[other * SEL : (other + 1) * SEL]
        for d in (2, 1, 3, 0):
            for other in (1, 0):
                if other or d:
                    chosen_copy(other, d).start()
        chosen_in[block_of * HALVES + core] = chosen[0]

    @pl.when(now < n_tm - 1)
    def _():
        halo.wait_recv()

    @pl.when(now == n_tm - 1)
    def _():
        halo_in[...] = jnp.zeros_like(halo_in)

    lay(halo_in, tiles)
    each(STATIONS // together, lambda g: prepare(g, 1))

    @pl.when(sends_part)
    def _():
        wait_for(chosen_in, PARTS - 1, sems.at[5])

    @pl.when(jnp.logical_not(sends_part))
    def _():
        wait_for(chosen_in, PARTS, sems.at[5])

    for b in range(WAVE_BLOCKS):
        halves = [chosen_in[b * HALVES + h].astype(f32) for h in range(HALVES)]
        chosen_all[:, b * LANES : (b + 1) * LANES] = halves[0] + halves[1]

    running[0] = jnp.zeros((tiles, LANES), f32)

    at_once = 20
    left_all = lax.broadcasted_iota(i32, (tiles, LANES), 1) < HALF_LANES

    def toeplitz_of(k):
        wide = jnp.broadcast_to(chosen_all[pl.ds(k, 1), :], (HALF_LANES, WAVE_BLOCKS * LANES))
        return pltpu.roll(wide, 0, 1, stride=1, stride_axis=0).astype(bf16)

    def correlate(group, total):
        numers = []
        for p in range(at_once * PER // 2):
            pair = group * (at_once * PER // 2) + p
            both = lax.dot_general(
                lhs[pair], jnp.concatenate([toeplitz_of(pair * 2), toeplitz_of(pair * 2 + 1)], axis=0),
                (((1,), (1,)), ((), ())), preferred_element_type=f32,
            )
            first, second, third, fourth = (both[i * tiles : (i + 1) * tiles] for i in range(4))
            swapped = pltpu.roll(jnp.where(left_all, second, third), HALF_LANES, 1)
            numers.append(jnp.where(left_all, first, swapped))
            numers.append(jnp.where(left_all, swapped, fourth))
        for u in range(at_once):
            station = group * at_once + u
            for d in range(PER):
                total = total + numers[u * PER + d] * scale[station, d]
            running[station + 1] = total
        return total

    lax.fori_loop(0, STATIONS // at_once, correlate, jnp.zeros((tiles, LANES), f32))

    def summed(template):
        return running[tab[1, template + 1] // PER] - running[tab[1, template] // PER]

    places = far_chips + [chip]
    share = len(places) // PAIR_PIECES

    def pair_copy(piece):
        span = pl.ds(piece * share, share)
        return pltpu.make_async_remote_copy(
            src_ref=pair_out.at[span], dst_ref=pair_in.at[span],
            send_sem=pair_sems.at[0, piece], recv_sem=pair_sems.at[1, piece],
            device_id=(sibling, now), device_id_type=MESH,
        )

    for piece in range(PAIR_PIECES):
        for i in range(piece * share, (piece + 1) * share):
            pair_out[i] = summed(places[i] * HALVES + 1 - core)
        pair_copy(piece).start()

    def stack_copy(place):
        return pltpu.make_async_remote_copy(
            src_ref=outgoing.at[place], dst_ref=incoming.at[chip],
            send_sem=sems.at[6], recv_sem=sems.at[7],
            device_id=(place * HALVES + core, now), device_id_type=MESH,
        )

    for i, place in enumerate(places):
        mine_out[i] = summed(place * HALVES + core)
    stack = jnp.zeros((tiles, LANES), f32)
    for i, place in enumerate(places):
        if i % share == 0:
            pair_copy(i // share).wait_recv()
        stack = mine_out[i] + pair_in[i]
        if i < len(far_chips):
            outgoing[place] = stack.astype(bf16)
            stack_copy(place).start()
    if far_chips:
        wait_for(incoming, len(far_chips), sems.at[7])
    for place in far_chips:
        stack = stack + incoming[place].astype(f32)
    stack_out[...] = stack
    peak_mine[...] = jnp.max(jnp.abs(stack), axis=0, keepdims=True)

    def peak_copy(i):
        return pltpu.make_async_remote_copy(
            src_ref=peak_mine, dst_ref=peak_in.at[now],
            send_sem=sems.at[8], recv_sem=sems.at[9],
            device_id=(me, tm_peer(i + 1)), device_id_type=MESH,
        )

    for i in range(n_tm - 1):
        peak_copy(i).start()
    wait_for(peak_in, n_tm - 1, sems.at[9])
    peak = peak_mine[...]
    for i in range(n_tm - 1):
        peak = jnp.maximum(peak, peak_in[tm_peer(i + 1)])
    peak_out[...] = jnp.broadcast_to(jnp.max(peak, axis=1, keepdims=True), peak_out.shape)

    @pl.when(now > 0)
    def _():
        halo.wait_send()

    @pl.when(sends_part)
    def _():
        wait_for(part_in, n_chan - 1, sems.at[2])
        wait_for(chosen_in, 2 * ROW - 1, sems.at[4])

    for piece in range(PAIR_PIECES):
        pair_copy(piece).wait_send()
    if far_chips:
        wait_for(outgoing, len(far_chips), sems.at[6])
    wait_for(peak_in, n_tm - 1, sems.at[8])


def on_device(n_chan, n_tm, seismic, waveforms, channel_list, moveouts):
    channels, piece = seismic.shape
    length = waveforms.shape[2]
    tiles = piece // LANES
    pitch = tiles + 8
    f32, bf16, i32 = jnp.float32, jnp.bfloat16, jnp.int32
    stack, peak = pl.pallas_call(
        functools.partial(kernel, n_chan, n_tm, length, channels),
        out_shape=(
            jax.ShapeDtypeStruct((tiles, LANES), f32),
            jax.ShapeDtypeStruct((8, LANES), f32),
        ),
        in_specs=[pl.BlockSpec(memory_space=pltpu.HBM)] * 4,
        out_specs=[pl.BlockSpec(memory_space=pltpu.VMEM)] * 2,
        scratch_shapes=[
            pltpu.VMEM(channel_list.shape, i32),
            pltpu.VMEM(moveouts.shape, i32),
            pltpu.VMEM((waveforms.shape[1], 1, length), f32),
            pltpu.VMEM((channels, piece), bf16),
            pltpu.VMEM((channels, HALO * LANES), bf16),
            pltpu.VMEM((8, LANES), i32),
            pltpu.SMEM((8, LANES), i32),
            pltpu.VMEM((channels, pitch, LANES), f32),
            pltpu.VMEM((4 * PER, tiles // 2 + 8, LANES), f32),
            pltpu.VMEM((SLOTS // 2, 4 * tiles, WAVE_BLOCKS * LANES), bf16),
            pltpu.VMEM((STATIONS, PER, tiles, LANES), f32),
            pltpu.VMEM((BLOCKS * LANES, LANES), bf16),
            pltpu.VMEM((32, WAVE_BLOCKS * LANES), bf16),
            pltpu.VMEM((n_chan, 16, LANES), bf16),
            pltpu.VMEM((2 * SEL, n_chan * 16), bf16),
            pltpu.VMEM((2, SEL, LANES), bf16),
            pltpu.VMEM((2 * ROW, SEL, LANES), bf16),
            pltpu.VMEM((SEL, WAVE_BLOCKS * LANES), f32),
            pltpu.VMEM((STATIONS + 1, tiles, LANES), f32),
            pltpu.VMEM((n_chan // HALVES, tiles, LANES), f32),
            pltpu.VMEM((n_chan // HALVES, tiles, LANES), f32),
            pltpu.VMEM((n_chan // HALVES, tiles, LANES), f32),
            pltpu.VMEM((n_chan // HALVES, tiles, LANES), bf16),
            pltpu.VMEM((n_chan // HALVES, tiles, LANES), bf16),
            pltpu.VMEM((1, LANES), f32),
            pltpu.VMEM((n_tm, 1, LANES), f32),
            pltpu.SemaphoreType.DMA((10,)),
            pltpu.SemaphoreType.DMA((2, PAIR_PIECES)),
            pltpu.SemaphoreType.DMA((5,)),
        ],
        compiler_params=pltpu.CompilerParams(
            collective_id=0, has_side_effects=True, vmem_limit_bytes=GRANT
        ),
    )(channel_list, moveouts, seismic, jnp.transpose(waveforms, (1, 0, 2)))
    return stack.reshape(1, piece), peak[0, 0:1]


def solution(mesh):
    return jax.shard_map(
        functools.partial(on_device, mesh.shape["chan"], mesh.shape["tm"]),
        mesh=mesh,
        in_specs=(P("chan", "tm"), P("chan", None, None), P(), P()),
        out_specs=(P("chan", "tm"), P("chan")),
        check_vma=False,
    )
```

```python
import functools
import math

import jax
import jax.numpy as jnp
from jax import lax
from jax.experimental import pallas as pl
from jax.experimental.pallas import tpu as pltpu
from jax.sharding import PartitionSpec as P

LANES = 128
HALF_LANES = 64
STATIONS = 20
PER = 3
SLOTS = STATIONS * PER
SEL = 64
HALO = 4
BLOCKS = 4
WAVE_BLOCKS = 3
HALVES = 2
PARTS = WAVE_BLOCKS * HALVES
ROW = 4
RING = 8
PAIR_PIECES = 2
DIRECT = 1
EPS = 1e-05
GRANT = 55200 * 1024
MESH = pl.DeviceIdType.MESH


def each(count, body, unroll=1):
    def step(i, carry):
        for u in range(unroll):
            body(i * unroll + u)
        return carry

    assert count % unroll == 0
    lax.fori_loop(0, count // unroll, step, 0)


def ring_offsets(n_chan):
    chips = n_chan // HALVES
    depth = min(RING, chips)
    offsets = [(dy, dz) for dy in range(chips // depth) for dz in range(depth)]
    return sorted(offsets, key=lambda o: (-(o[0] + min(o[1], depth - o[1])), o))


def before(x, axis):
    index = lax.broadcasted_iota(jnp.int32, x.shape, axis)
    step, total = 1, x
    while step < 32:
        total = total + jnp.where(index >= step, pltpu.roll(total, step, axis), 0)
        step *= 2
    return total - x


def kernel(
    n_chan, n_tm, length, channels,
    listed, moves, seis, waves,
    stack_out, peak_out,
    listed_in, moves_in, waves_in, x_in, halo_in, tab_v, tab,
    rows, turned, lhs, scale, band,
    normed, part_in, takes, chosen, chosen_in, chosen_all,
    running, mine_out, pair_out, pair_in, outgoing, incoming, peak_mine, peak_in,
    sems, pair_sems, in_sems,
):
    me = lax.axis_index("chan")
    now = lax.axis_index("tm")
    core = lax.rem(me, HALVES)
    across = lax.rem(now, ROW)
    row_start = now - across
    sibling = me + 1 - 2 * core
    tiles = stack_out.shape[0]
    pitch = rows.shape[1]
    flat_rows = rows.reshape(channels * pitch, LANES)
    half_tiles = tiles // 2
    f32, bf16, i32 = jnp.float32, jnp.bfloat16, jnp.int32

    def wait_for(ref, blocks, sem):
        span = ref.at[pl.ds(0, blocks)]
        pltpu.make_async_copy(span, span, sem).wait()

    chip = me // HALVES
    depth = min(RING, n_chan // HALVES)
    offsets = ring_offsets(n_chan)

    def chip_at(offset):
        dy, dz = offset
        y, z = chip // depth, lax.rem(chip, depth)
        return lax.rem(y + dy, n_chan // HALVES // depth) * depth + lax.rem(z + dz, depth)

    chan_peers = [
        chip_at(offset) * HALVES + lax.rem(core + dc, HALVES)
        for offset in offsets for dc in range(HALVES) if offset != (0, 0) or dc
    ]
    far_chips = [chip_at(offset) for offset in offsets if offset != (0, 0)]

    def tm_peer(d):
        return lax.rem(now + d, n_tm)

    def row_peer(d):
        return row_start + lax.rem(across + d, ROW)

    barrier = pltpu.get_barrier_semaphore()

    loads = [
        pltpu.make_async_copy(src, dst, in_sems.at[i])
        for i, (src, dst) in enumerate(
            ((waves, waves_in), (listed, listed_in), (moves, moves_in), (seis, x_in))
        )
    ]
    loads[0].start()

    def greet(group, piece):
        pl.semaphore_signal(barrier, inc=1, device_id=(group, piece), device_id_type=MESH)

    for peer in chan_peers[: n_chan // 2]:
        greet(peer, now)
    for i in range(n_tm - 1):
        greet(me, tm_peer(i + 1))
    for i in range(ROW - 1):
        greet(sibling, row_peer(i + 1))
    for peer in chan_peers[n_chan // 2 :]:
        greet(peer, now)

    for copy in loads[1:]:
        copy.start()

    loads[0].wait()
    w = waves_in[:, 0, :]
    centered = w - jnp.mean(w, axis=-1, keepdims=True)
    factor = lax.rsqrt(jnp.mean(centered * centered, axis=-1, keepdims=True) + EPS) / math.sqrt(length)
    normed[...] = jnp.zeros_like(normed)
    normed[0 : w.shape[0], 0:length] = (centered * factor).astype(bf16)

    pl.semaphore_wait(barrier, n_chan - 1 + n_tm - 1 + ROW - 1)

    halo = pltpu.make_async_remote_copy(
        src_ref=seis.at[:, pl.ds(0, HALO * LANES)], dst_ref=halo_in,
        send_sem=sems.at[0], recv_sem=sems.at[1],
        device_id=(me, jnp.maximum(now - 1, 0)), device_id_type=MESH,
    )

    sends_part = across < WAVE_BLOCKS
    block_of = jnp.minimum(across, WAVE_BLOCKS - 1)

    def part(half):
        return normed.at[pl.ds(half * 16, 16), pl.ds(block_of * LANES, LANES)]

    def part_copy(peer):
        return pltpu.make_async_remote_copy(
            src_ref=part(lax.rem(peer, HALVES)), dst_ref=part_in.at[me],
            send_sem=sems.at[2], recv_sem=sems.at[3],
            device_id=(peer, now), device_id_type=MESH,
        )

    @pl.when(sends_part)
    def _():
        for peer in chan_peers:
            part_copy(peer).start()
        part_in[me] = part(core)[...]

    @pl.when(now > 0)
    def _():
        halo.start()

    lag = lax.broadcasted_iota(i32, band.shape, 0) - lax.broadcasted_iota(i32, band.shape, 1)
    band[...] = jnp.where((lag >= 0) & (lag < length), 1.0, 0.0).astype(bf16)

    loads[1].wait()
    loads[2].wait()
    templates, per_template = listed_in.shape
    names = listed_in[...]
    column = lax.broadcasted_iota(i32, names.shape, 1)
    key = jnp.full(names.shape, -1, i32)
    code = (lax.broadcasted_iota(i32, names.shape, 0) * 32 + column) * LANES + moves_in[...]
    counts = jnp.zeros((templates, 1), i32)
    for place, group in ((0, me), (SEL, sibling)):
        from_first = names - group * channels
        inside = (from_first >= 0) & (from_first < channels)
        mine = jnp.where(inside, 1, 0)
        in_row = before(mine, 1)
        full_row = jnp.sum(mine, axis=1, keepdims=True)
        rank = in_row + before(jnp.broadcast_to(full_row, mine.shape), 0)
        key = jnp.where(inside & (rank < SLOTS), rank + place, key)
        code = jnp.where(inside, code + from_first * (1 << 17), code)
        if place == 0:
            counts = full_row
    lane32 = lax.broadcasted_iota(i32, (templates, LANES), 1)
    found = jnp.zeros((templates, LANES), i32)
    for c in range(per_template):
        found = found + jnp.where(
            lane32 == jnp.broadcast_to(key[:, c : c + 1], lane32.shape),
            jnp.broadcast_to(code[:, c : c + 1], lane32.shape), 0,
        )
    ahead = jnp.where(
        lax.broadcasted_iota(i32, lane32.shape, 0) < lane32, jnp.broadcast_to(counts, lane32.shape), 0
    )
    tab_v[0:1, :] = jnp.sum(found, axis=0, keepdims=True)
    tab_v[1:2, :] = jnp.minimum(jnp.sum(ahead, axis=0, keepdims=True), SLOTS)
    to_scalars = pltpu.make_async_copy(tab_v, tab, in_sems.at[4])
    to_scalars.start()

    def lay(ref, first):
        for i in range(ref.shape[1] // LANES):
            for c in range(0, channels, 16):
                flat_rows[pl.ds(c * pitch + first + i, 16, stride=pitch), :] = ref[
                    c : c + 16, i * LANES : (i + 1) * LANES
                ].astype(f32)

    loads[3].wait()
    lay(x_in, 0)
    to_scalars.wait()

    entries = tab_v[0:1, :]
    rows_of = (entries >> 7) & 31
    taken = jnp.where(rows_of // 16 == core, ((entries >> 12) & 31) * 16 + rows_of % 16, -1)
    taken = jnp.broadcast_to(taken, (n_chan * 16, LANES))
    hot = jnp.where(lax.broadcasted_iota(i32, taken.shape, 0) == taken, 1.0, 0.0)
    for b in range(n_chan * 16 // LANES):
        takes[:, b * LANES : (b + 1) * LANES] = hot[b * LANES : (b + 1) * LANES].T.astype(bf16)

    lane = lax.broadcasted_iota(i32, (half_tiles, LANES), 1)
    left = lane < HALF_LANES
    together = 4

    def prepare(group, half):
        squares = []
        first = half * half_tiles
        for u in range(together):
            station = group * together + u
            for d in range(PER):
                entry = tab[0, station * PER + d]
                move = entry & (LANES - 1)
                record = rows[entry >> 17][first : first + half_tiles + 8]
                at = u * PER + d
                turned[at] = pltpu.roll(record, lax.rem(LANES - move, LANES), 1)
                here = lane < LANES - move
                parts = [turned[at, b : b + half_tiles, :] for b in range(BLOCKS + 1)]
                shifted = [jnp.where(here, parts[b], parts[b + 1]) for b in range(BLOCKS)]
                swung = [pltpu.roll(s, HALF_LANES, 1) for s in shifted]
                later = [jnp.where(left, swung[b], swung[b + 1]) for b in range(WAVE_BLOCKS)]
                for phase, tile in enumerate((shifted[:WAVE_BLOCKS], later)):
                    at_row = (at % 2 * 2 + phase) * tiles + first
                    lhs[group * (together * PER // 2) + at // 2, at_row : at_row + half_tiles, :] = jnp.concatenate(
                        [s.astype(bf16) for s in tile], axis=1
                    )
                squares.append(jnp.concatenate([(s * s).astype(bf16) for s in shifted], axis=1))
        energy = jnp.dot(jnp.concatenate(squares, axis=0), band[...], preferred_element_type=f32)
        factor = lax.rsqrt(energy / length + EPS) / math.sqrt(length)
        for u in range(together):
            for d in range(PER):
                at = (u * PER + d) * half_tiles
                scale[group * together + u, d, first : first + half_tiles, :] = factor[at : at + half_tiles]

    each(STATIONS // together, lambda g: prepare(g, 0))

    def chosen_copy(other, d):
        return pltpu.make_async_remote_copy(
            src_ref=chosen.at[other], dst_ref=chosen_in.at[block_of * HALVES + core],
            send_sem=sems.at[4], recv_sem=sems.at[5],
            device_id=(sibling if other else me, row_peer(d)), device_id_type=MESH,
        )

    @pl.when(sends_part)
    def _():
        wait_for(part_in, n_chan - 1, sems.at[3])
        picked = jnp.dot(
            takes[...], part_in[...].reshape(n_chan * 16, LANES), preferred_element_type=f32
        ).astype(bf16)
        for other in (1, 0):
            chosen[other] = picked[other * SEL : (other + 1) * SEL]
        for d in (2, 1, 3, 0):
            for other in (1, 0):
                if other or d:
                    chosen_copy(other, d).start()
        chosen_in[block_of * HALVES + core] = chosen[0]

    @pl.when(now < n_tm - 1)
    def _():
        halo.wait_recv()

    @pl.when(now == n_tm - 1)
    def _():
        halo_in[...] = jnp.zeros_like(halo_in)

    lay(halo_in, tiles)
    each(STATIONS // together, lambda g: prepare(g, 1))

    @pl.when(sends_part)
    def _():
        wait_for(chosen_in, PARTS - 1, sems.at[5])

    @pl.when(jnp.logical_not(sends_part))
    def _():
        wait_for(chosen_in, PARTS, sems.at[5])

    for b in range(WAVE_BLOCKS):
        halves = [chosen_in[b * HALVES + h].astype(f32) for h in range(HALVES)]
        chosen_all[:, b * LANES : (b + 1) * LANES] = halves[0] + halves[1]

    running[0] = jnp.zeros((tiles, LANES), f32)

    at_once = 20
    left_all = lax.broadcasted_iota(i32, (tiles, LANES), 1) < HALF_LANES

    def toeplitz_of(k):
        wide = jnp.broadcast_to(chosen_all[pl.ds(k, 1), :], (HALF_LANES, WAVE_BLOCKS * LANES))
        return pltpu.roll(wide, 0, 1, stride=1, stride_axis=0).astype(bf16)

    def correlate(group, total):
        numers = []
        for p in range(at_once * PER // 2):
            pair = group * (at_once * PER // 2) + p
            both = lax.dot_general(
                lhs[pair], jnp.concatenate([toeplitz_of(pair * 2), toeplitz_of(pair * 2 + 1)], axis=0),
                (((1,), (1,)), ((), ())), preferred_element_type=f32,
            )
            first, second, third, fourth = (both[i * tiles : (i + 1) * tiles] for i in range(4))
            swapped = pltpu.roll(jnp.where(left_all, second, third), HALF_LANES, 1)
            numers.append(jnp.where(left_all, first, swapped))
            numers.append(jnp.where(left_all, swapped, fourth))
        for u in range(at_once):
            station = group * at_once + u
            for d in range(PER):
                total = total + numers[u * PER + d] * scale[station, d]
            running[station + 1] = total
        return total

    lax.fori_loop(0, STATIONS // at_once, correlate, jnp.zeros((tiles, LANES), f32))

    def summed(template):
        return running[tab[1, template + 1] // PER] - running[tab[1, template] // PER]

    def stack_copy(peer):
        return pltpu.make_async_remote_copy(
            src_ref=outgoing.at[peer], dst_ref=incoming.at[me],
            send_sem=sems.at[6], recv_sem=sems.at[7],
            device_id=(peer, now), device_id_type=MESH,
        )

    def send_stack(peer, total):
        outgoing[peer] = total.astype(bf16)
        stack_copy(peer).start()

    direct = far_chips[:DIRECT]
    for place in direct:
        for c in range(HALVES):
            send_stack(place * HALVES + c, summed(place * HALVES + c))

    places = far_chips[len(direct) :] + [chip]
    cuts = [0, (len(places) + 1) // 2, len(places)]

    def pair_copy(piece):
        span = pl.ds(cuts[piece], cuts[piece + 1] - cuts[piece])
        return pltpu.make_async_remote_copy(
            src_ref=pair_out.at[span], dst_ref=pair_in.at[span],
            send_sem=pair_sems.at[0, piece], recv_sem=pair_sems.at[1, piece],
            device_id=(sibling, now), device_id_type=MESH,
        )

    for piece in range(PAIR_PIECES):
        for i in range(cuts[piece], cuts[piece + 1]):
            pair_out[i] = summed(places[i] * HALVES + 1 - core)
        pair_copy(piece).start()
    for i, place in enumerate(places):
        mine_out[i] = summed(place * HALVES + core)
    stack = jnp.zeros((tiles, LANES), f32)
    for i, place in enumerate(places):
        if i in cuts:
            pair_copy(cuts.index(i)).wait_recv()
        stack = mine_out[i] + pair_in[i]
        if i < len(places) - 1:
            send_stack(place * HALVES + core, stack)
    received = [place * HALVES + c for place in direct for c in range(HALVES)]
    received += [place * HALVES + core for place in places[:-1]]
    wait_for(incoming, len(received), sems.at[7])
    for peer in received:
        stack = stack + incoming[peer].astype(f32)
    stack_out[...] = stack
    peak_mine[...] = jnp.max(jnp.abs(stack), axis=0, keepdims=True)

    def peak_copy(i):
        return pltpu.make_async_remote_copy(
            src_ref=peak_mine, dst_ref=peak_in.at[now],
            send_sem=sems.at[8], recv_sem=sems.at[9],
            device_id=(me, tm_peer(i + 1)), device_id_type=MESH,
        )

    for i in range(n_tm - 1):
        peak_copy(i).start()
    wait_for(peak_in, n_tm - 1, sems.at[9])
    peak = peak_mine[...]
    for i in range(n_tm - 1):
        peak = jnp.maximum(peak, peak_in[tm_peer(i + 1)])
    peak_out[...] = jnp.broadcast_to(jnp.max(peak, axis=1, keepdims=True), peak_out.shape)

    @pl.when(now > 0)
    def _():
        halo.wait_send()

    @pl.when(sends_part)
    def _():
        wait_for(part_in, n_chan - 1, sems.at[2])
        wait_for(chosen_in, 2 * ROW - 1, sems.at[4])

    for piece in range(PAIR_PIECES):
        pair_copy(piece).wait_send()
    wait_for(outgoing, len(received), sems.at[6])
    wait_for(peak_in, n_tm - 1, sems.at[8])


def on_device(n_chan, n_tm, seismic, waveforms, channel_list, moveouts):
    channels, piece = seismic.shape
    length = waveforms.shape[2]
    tiles = piece // LANES
    pitch = tiles + 8
    f32, bf16, i32 = jnp.float32, jnp.bfloat16, jnp.int32
    stack, peak = pl.pallas_call(
        functools.partial(kernel, n_chan, n_tm, length, channels),
        out_shape=(
            jax.ShapeDtypeStruct((tiles, LANES), f32),
            jax.ShapeDtypeStruct((8, LANES), f32),
        ),
        in_specs=[pl.BlockSpec(memory_space=pltpu.HBM)] * 4,
        out_specs=[pl.BlockSpec(memory_space=pltpu.VMEM)] * 2,
        scratch_shapes=[
            pltpu.VMEM(channel_list.shape, i32),
            pltpu.VMEM(moveouts.shape, i32),
            pltpu.VMEM((waveforms.shape[1], 1, length), f32),
            pltpu.VMEM((channels, piece), bf16),
            pltpu.VMEM((channels, HALO * LANES), bf16),
            pltpu.VMEM((8, LANES), i32),
            pltpu.SMEM((8, LANES), i32),
            pltpu.VMEM((channels, pitch, LANES), f32),
            pltpu.VMEM((4 * PER, tiles // 2 + 8, LANES), f32),
            pltpu.VMEM((SLOTS // 2, 4 * tiles, WAVE_BLOCKS * LANES), bf16),
            pltpu.VMEM((STATIONS, PER, tiles, LANES), f32),
            pltpu.VMEM((BLOCKS * LANES, LANES), bf16),
            pltpu.VMEM((32, WAVE_BLOCKS * LANES), bf16),
            pltpu.VMEM((n_chan, 16, LANES), bf16),
            pltpu.VMEM((2 * SEL, n_chan * 16), bf16),
            pltpu.VMEM((2, SEL, LANES), bf16),
            pltpu.VMEM((2 * ROW, SEL, LANES), bf16),
            pltpu.VMEM((SEL, WAVE_BLOCKS * LANES), f32),
            pltpu.VMEM((STATIONS + 1, tiles, LANES), f32),
            pltpu.VMEM((n_chan // HALVES, tiles, LANES), f32),
            pltpu.VMEM((n_chan // HALVES, tiles, LANES), f32),
            pltpu.VMEM((n_chan // HALVES, tiles, LANES), f32),
            pltpu.VMEM((n_chan, tiles, LANES), bf16),
            pltpu.VMEM((n_chan, tiles, LANES), bf16),
            pltpu.VMEM((1, LANES), f32),
            pltpu.VMEM((n_tm, 1, LANES), f32),
            pltpu.SemaphoreType.DMA((10,)),
            pltpu.SemaphoreType.DMA((2, PAIR_PIECES)),
            pltpu.SemaphoreType.DMA((5,)),
        ],
        compiler_params=pltpu.CompilerParams(
            collective_id=0, has_side_effects=True, vmem_limit_bytes=GRANT
        ),
    )(channel_list, moveouts, seismic, jnp.transpose(waveforms, (1, 0, 2)))
    return stack.reshape(1, piece), peak[0, 0:1]


def solution(mesh):
    return jax.shard_map(
        functools.partial(on_device, mesh.shape["chan"], mesh.shape["tm"]),
        mesh=mesh,
        in_specs=(P("chan", "tm"), P("chan", None, None), P(), P()),
        out_specs=(P("chan", "tm"), P("chan")),
        check_vma=False,
    )
```

```python
import functools
import math

import jax
import jax.numpy as jnp
from jax import lax
from jax.experimental import pallas as pl
from jax.experimental.pallas import tpu as pltpu
from jax.sharding import PartitionSpec as P

LANES = 128
HALF_LANES = 64
STATIONS = 20
PER = 3
SLOTS = STATIONS * PER
SEL = 64
HALO = 4
BLOCKS = 4
WAVE_BLOCKS = 3
HALVES = 2
PARTS = WAVE_BLOCKS * HALVES
ROW = 4
RING = 8
PAIR_PIECES = 2
EPS = 1e-05
GRANT = 55200 * 1024
MESH = pl.DeviceIdType.MESH


def each(count, body, unroll=1):
    def step(i, carry):
        for u in range(unroll):
            body(i * unroll + u)
        return carry

    assert count % unroll == 0
    lax.fori_loop(0, count // unroll, step, 0)


def ring_offsets(n_chan):
    chips = n_chan // HALVES
    depth = min(RING, chips)
    offsets = [(dy, dz) for dy in range(chips // depth) for dz in range(depth)]
    return sorted(offsets, key=lambda o: (-(o[0] + min(o[1], depth - o[1])), o))


def before(x, axis):
    index = lax.broadcasted_iota(jnp.int32, x.shape, axis)
    step, total = 1, x
    while step < 32:
        total = total + jnp.where(index >= step, pltpu.roll(total, step, axis), 0)
        step *= 2
    return total - x


def kernel(
    n_chan, n_tm, length, channels,
    listed, moves, seis, waves,
    stack_out, peak_out,
    listed_in, moves_in, waves_in, x_in, halo_in, tab_v, tab,
    rows, turned, lhs, scale, band,
    normed, part_in, takes, chosen, chosen_in, chosen_all,
    running, mine_out, pair_out, pair_in, outgoing, incoming, peak_mine, peak_in,
    sems, pair_sems, in_sems,
):
    me = lax.axis_index("chan")
    now = lax.axis_index("tm")
    core = lax.rem(me, HALVES)
    across = lax.rem(now, ROW)
    row_start = now - across
    sibling = me + 1 - 2 * core
    tiles = stack_out.shape[0]
    pitch = rows.shape[1]
    flat_rows = rows.reshape(channels * pitch, LANES)
    half_tiles = tiles // 2
    f32, bf16, i32 = jnp.float32, jnp.bfloat16, jnp.int32

    def wait_for(ref, blocks, sem):
        span = ref.at[pl.ds(0, blocks)]
        pltpu.make_async_copy(span, span, sem).wait()

    chip = me // HALVES
    depth = min(RING, n_chan // HALVES)
    offsets = ring_offsets(n_chan)

    def chip_at(offset):
        dy, dz = offset
        y, z = chip // depth, lax.rem(chip, depth)
        return lax.rem(y + dy, n_chan // HALVES // depth) * depth + lax.rem(z + dz, depth)

    chan_peers = [
        chip_at(offset) * HALVES + lax.rem(core + dc, HALVES)
        for offset in offsets for dc in range(HALVES) if offset != (0, 0) or dc
    ]
    far_chips = [chip_at(offset) for offset in offsets if offset != (0, 0)]

    def tm_peer(d):
        return lax.rem(now + d, n_tm)

    def row_peer(d):
        return row_start + lax.rem(across + d, ROW)

    barrier = pltpu.get_barrier_semaphore()

    loads = [
        pltpu.make_async_copy(src, dst, in_sems.at[i])
        for i, (src, dst) in enumerate(
            ((waves, waves_in), (listed, listed_in), (moves, moves_in), (seis, x_in))
        )
    ]
    loads[0].start()

    def greet(group, piece):
        pl.semaphore_signal(barrier, inc=1, device_id=(group, piece), device_id_type=MESH)

    for peer in chan_peers[: n_chan // 2]:
        greet(peer, now)
    for i in range(n_tm - 1):
        greet(me, tm_peer(i + 1))
    for i in range(ROW - 1):
        greet(sibling, row_peer(i + 1))
    for peer in chan_peers[n_chan // 2 :]:
        greet(peer, now)

    for copy in loads[1:]:
        copy.start()

    loads[0].wait()
    w = waves_in[:, 0, :]
    centered = w - jnp.mean(w, axis=-1, keepdims=True)
    factor = lax.rsqrt(jnp.mean(centered * centered, axis=-1, keepdims=True) + EPS) / math.sqrt(length)
    normed[...] = jnp.zeros_like(normed)
    normed[0 : w.shape[0], 0:length] = (centered * factor).astype(bf16)

    pl.semaphore_wait(barrier, n_chan - 1 + n_tm - 1 + ROW - 1)

    halo = pltpu.make_async_remote_copy(
        src_ref=seis.at[:, pl.ds(0, HALO * LANES)], dst_ref=halo_in,
        send_sem=sems.at[0], recv_sem=sems.at[1],
        device_id=(me, jnp.maximum(now - 1, 0)), device_id_type=MESH,
    )

    sends_part = across < WAVE_BLOCKS
    block_of = jnp.minimum(across, WAVE_BLOCKS - 1)

    def part(half):
        return normed.at[pl.ds(half * 16, 16), pl.ds(block_of * LANES, LANES)]

    def part_copy(peer):
        return pltpu.make_async_remote_copy(
            src_ref=part(lax.rem(peer, HALVES)), dst_ref=part_in.at[me],
            send_sem=sems.at[2], recv_sem=sems.at[3],
            device_id=(peer, now), device_id_type=MESH,
        )

    @pl.when(sends_part)
    def _():
        for peer in chan_peers:
            part_copy(peer).start()
        part_in[me] = part(core)[...]

    @pl.when(now > 0)
    def _():
        halo.start()

    lag = lax.broadcasted_iota(i32, band.shape, 0) - lax.broadcasted_iota(i32, band.shape, 1)
    band[...] = jnp.where((lag >= 0) & (lag < length), 1.0, 0.0).astype(bf16)

    loads[1].wait()
    loads[2].wait()
    templates, per_template = listed_in.shape
    names = listed_in[...]
    column = lax.broadcasted_iota(i32, names.shape, 1)
    key = jnp.full(names.shape, -1, i32)
    code = (lax.broadcasted_iota(i32, names.shape, 0) * 32 + column) * LANES + moves_in[...]
    counts = jnp.zeros((templates, 1), i32)
    for place, group in ((0, me), (SEL, sibling)):
        from_first = names - group * channels
        inside = (from_first >= 0) & (from_first < channels)
        mine = jnp.where(inside, 1, 0)
        in_row = before(mine, 1)
        full_row = jnp.sum(mine, axis=1, keepdims=True)
        rank = in_row + before(jnp.broadcast_to(full_row, mine.shape), 0)
        key = jnp.where(inside & (rank < SLOTS), rank + place, key)
        code = jnp.where(inside, code + from_first * (1 << 17), code)
        if place == 0:
            counts = full_row
    lane32 = lax.broadcasted_iota(i32, (templates, LANES), 1)
    found = jnp.zeros((templates, LANES), i32)
    for c in range(per_template):
        found = found + jnp.where(
            lane32 == jnp.broadcast_to(key[:, c : c + 1], lane32.shape),
            jnp.broadcast_to(code[:, c : c + 1], lane32.shape), 0,
        )
    ahead = jnp.where(
        lax.broadcasted_iota(i32, lane32.shape, 0) < lane32, jnp.broadcast_to(counts, lane32.shape), 0
    )
    tab_v[0:1, :] = jnp.sum(found, axis=0, keepdims=True)
    tab_v[1:2, :] = jnp.minimum(jnp.sum(ahead, axis=0, keepdims=True), SLOTS)
    to_scalars = pltpu.make_async_copy(tab_v, tab, in_sems.at[4])
    to_scalars.start()

    def lay(ref, first):
        for i in range(ref.shape[1] // LANES):
            for c in range(0, channels, 16):
                flat_rows[pl.ds(c * pitch + first + i, 16, stride=pitch), :] = ref[
                    c : c + 16, i * LANES : (i + 1) * LANES
                ].astype(f32)

    loads[3].wait()
    lay(x_in, 0)
    to_scalars.wait()

    entries = tab_v[0:1, :]
    rows_of = (entries >> 7) & 31
    taken = jnp.where(rows_of // 16 == core, ((entries >> 12) & 31) * 16 + rows_of % 16, -1)
    taken = jnp.broadcast_to(taken, (n_chan * 16, LANES))
    hot = jnp.where(lax.broadcasted_iota(i32, taken.shape, 0) == taken, 1.0, 0.0)
    for b in range(n_chan * 16 // LANES):
        takes[:, b * LANES : (b + 1) * LANES] = hot[b * LANES : (b + 1) * LANES].T.astype(bf16)

    lane = lax.broadcasted_iota(i32, (half_tiles, LANES), 1)
    left = lane < HALF_LANES
    together = 4

    def prepare(group, half):
        squares = []
        first = half * half_tiles
        for u in range(together):
            station = group * together + u
            for d in range(PER):
                entry = tab[0, station * PER + d]
                move = entry & (LANES - 1)
                record = rows[entry >> 17][first : first + half_tiles + 8]
                at = u * PER + d
                turned[at] = pltpu.roll(record, lax.rem(LANES - move, LANES), 1)
                here = lane < LANES - move
                parts = [turned[at, b : b + half_tiles, :] for b in range(BLOCKS + 1)]
                shifted = [jnp.where(here, parts[b], parts[b + 1]) for b in range(BLOCKS)]
                swung = [pltpu.roll(s, HALF_LANES, 1) for s in shifted]
                later = [jnp.where(left, swung[b], swung[b + 1]) for b in range(WAVE_BLOCKS)]
                for phase, tile in enumerate((shifted[:WAVE_BLOCKS], later)):
                    at_row = (at % 2 * 2 + phase) * tiles + first
                    lhs[group * (together * PER // 2) + at // 2, at_row : at_row + half_tiles, :] = jnp.concatenate(
                        [s.astype(bf16) for s in tile], axis=1
                    )
                squares.append(jnp.concatenate([(s * s).astype(bf16) for s in shifted], axis=1))
        energy = jnp.dot(jnp.concatenate(squares, axis=0), band[...], preferred_element_type=f32)
        factor = lax.rsqrt(energy / length + EPS) / math.sqrt(length)
        for u in range(together):
            for d in range(PER):
                at = (u * PER + d) * half_tiles
                scale[group * together + u, d, first : first + half_tiles, :] = factor[at : at + half_tiles]

    each(STATIONS // together, lambda g: prepare(g, 0))

    def chosen_copy(other, d):
        return pltpu.make_async_remote_copy(
            src_ref=chosen.at[other], dst_ref=chosen_in.at[block_of * HALVES + core],
            send_sem=sems.at[4], recv_sem=sems.at[5],
            device_id=(sibling if other else me, row_peer(d)), device_id_type=MESH,
        )

    @pl.when(sends_part)
    def _():
        wait_for(part_in, n_chan - 1, sems.at[3])
        picked = jnp.dot(
            takes[...], part_in[...].reshape(n_chan * 16, LANES), preferred_element_type=f32
        ).astype(bf16)
        for other in (1, 0):
            chosen[other] = picked[other * SEL : (other + 1) * SEL]
        for d in (2, 1, 3, 0):
            for other in (1, 0):
                if other or d:
                    chosen_copy(other, d).start()
        chosen_in[block_of * HALVES + core] = chosen[0]

    @pl.when(now < n_tm - 1)
    def _():
        halo.wait_recv()

    @pl.when(now == n_tm - 1)
    def _():
        halo_in[...] = jnp.zeros_like(halo_in)

    lay(halo_in, tiles)
    each(STATIONS // together, lambda g: prepare(g, 1))

    @pl.when(sends_part)
    def _():
        wait_for(chosen_in, PARTS - 1, sems.at[5])

    @pl.when(jnp.logical_not(sends_part))
    def _():
        wait_for(chosen_in, PARTS, sems.at[5])

    for b in range(WAVE_BLOCKS):
        halves = [chosen_in[b * HALVES + h].astype(f32) for h in range(HALVES)]
        chosen_all[:, b * LANES : (b + 1) * LANES] = halves[0] + halves[1]

    running[0] = jnp.zeros((tiles, LANES), f32)

    at_once = 20
    left_all = lax.broadcasted_iota(i32, (tiles, LANES), 1) < HALF_LANES

    def toeplitz_of(k):
        wide = jnp.broadcast_to(chosen_all[pl.ds(k, 1), :], (HALF_LANES, WAVE_BLOCKS * LANES))
        return pltpu.roll(wide, 0, 1, stride=1, stride_axis=0).astype(bf16)

    def correlate(group, total):
        numers = []
        for p in range(at_once * PER // 4):
            quad = group * (at_once * PER // 4) + p
            wide = lax.dot_general(
                lhs[pl.ds(quad * 2, 2)].reshape(8 * tiles, WAVE_BLOCKS * LANES),
                jnp.concatenate([toeplitz_of(quad * 4 + i) for i in range(4)], axis=0),
                (((1,), (1,)), ((), ())), preferred_element_type=f32,
            )
            for h in range(2):
                both = wide[h * 4 * tiles : (h + 1) * 4 * tiles, h * LANES : (h + 1) * LANES]
                first, second, third, fourth = (both[i * tiles : (i + 1) * tiles] for i in range(4))
                swapped = pltpu.roll(jnp.where(left_all, second, third), HALF_LANES, 1)
                numers.append(jnp.where(left_all, first, swapped))
                numers.append(jnp.where(left_all, swapped, fourth))
        for u in range(at_once):
            station = group * at_once + u
            for d in range(PER):
                total = total + numers[u * PER + d] * scale[station, d]
            running[station + 1] = total
        return total

    lax.fori_loop(0, STATIONS // at_once, correlate, jnp.zeros((tiles, LANES), f32))

    def summed(template):
        return running[tab[1, template + 1] // PER] - running[tab[1, template] // PER]

    places = far_chips + [chip]
    share = len(places) // PAIR_PIECES

    def pair_copy(piece):
        span = pl.ds(piece * share, share)
        return pltpu.make_async_remote_copy(
            src_ref=pair_out.at[span], dst_ref=pair_in.at[span],
            send_sem=pair_sems.at[0, piece], recv_sem=pair_sems.at[1, piece],
            device_id=(sibling, now), device_id_type=MESH,
        )

    for piece in range(PAIR_PIECES):
        for i in range(piece * share, (piece + 1) * share):
            pair_out[i] = summed(places[i] * HALVES + 1 - core)
        pair_copy(piece).start()

    def stack_copy(place):
        return pltpu.make_async_remote_copy(
            src_ref=outgoing.at[place], dst_ref=incoming.at[chip],
            send_sem=sems.at[6], recv_sem=sems.at[7],
            device_id=(place * HALVES + core, now), device_id_type=MESH,
        )

    for i, place in enumerate(places):
        mine_out[i] = summed(place * HALVES + core)
    stack = jnp.zeros((tiles, LANES), f32)
    for i, place in enumerate(places):
        if i % share == 0:
            pair_copy(i // share).wait_recv()
        stack = mine_out[i] + pair_in[i]
        if i < len(far_chips):
            outgoing[place] = stack.astype(bf16)
            stack_copy(place).start()
    if far_chips:
        wait_for(incoming, len(far_chips), sems.at[7])
    for place in far_chips:
        stack = stack + incoming[place].astype(f32)
    stack_out[...] = stack
    peak_mine[...] = jnp.max(jnp.abs(stack).reshape(tiles // 8, 8, LANES), axis=0)

    def peak_copy(i):
        return pltpu.make_async_remote_copy(
            src_ref=peak_mine, dst_ref=peak_in.at[now],
            send_sem=sems.at[8], recv_sem=sems.at[9],
            device_id=(me, tm_peer(i + 1)), device_id_type=MESH,
        )

    for i in range(n_tm - 1):
        peak_copy(i).start()
    wait_for(peak_in, n_tm - 1, sems.at[9])
    peak = peak_mine[...]
    for i in range(n_tm - 1):
        peak = jnp.maximum(peak, peak_in[tm_peer(i + 1)])
    peak_out[...] = peak

    @pl.when(now > 0)
    def _():
        halo.wait_send()

    @pl.when(sends_part)
    def _():
        wait_for(part_in, n_chan - 1, sems.at[2])
        wait_for(chosen_in, 2 * ROW - 1, sems.at[4])

    for piece in range(PAIR_PIECES):
        pair_copy(piece).wait_send()
    if far_chips:
        wait_for(outgoing, len(far_chips), sems.at[6])
    wait_for(peak_in, n_tm - 1, sems.at[8])


def on_device(n_chan, n_tm, seismic, waveforms, channel_list, moveouts):
    channels, piece = seismic.shape
    length = waveforms.shape[2]
    tiles = piece // LANES
    pitch = tiles + 8
    f32, bf16, i32 = jnp.float32, jnp.bfloat16, jnp.int32
    stack, peak = pl.pallas_call(
        functools.partial(kernel, n_chan, n_tm, length, channels),
        out_shape=(
            jax.ShapeDtypeStruct((tiles, LANES), f32),
            jax.ShapeDtypeStruct((8, LANES), f32),
        ),
        in_specs=[pl.BlockSpec(memory_space=pltpu.HBM)] * 4,
        out_specs=[pl.BlockSpec(memory_space=pltpu.VMEM)] * 2,
        scratch_shapes=[
            pltpu.VMEM(channel_list.shape, i32),
            pltpu.VMEM(moveouts.shape, i32),
            pltpu.VMEM((waveforms.shape[1], 1, length), f32),
            pltpu.VMEM((channels, piece), bf16),
            pltpu.VMEM((channels, HALO * LANES), bf16),
            pltpu.VMEM((8, LANES), i32),
            pltpu.SMEM((8, LANES), i32),
            pltpu.VMEM((channels, pitch, LANES), f32),
            pltpu.VMEM((4 * PER, tiles // 2 + 8, LANES), f32),
            pltpu.VMEM((SLOTS // 2, 4 * tiles, WAVE_BLOCKS * LANES), bf16),
            pltpu.VMEM((STATIONS, PER, tiles, LANES), f32),
            pltpu.VMEM((BLOCKS * LANES, LANES), bf16),
            pltpu.VMEM((32, WAVE_BLOCKS * LANES), bf16),
            pltpu.VMEM((n_chan, 16, LANES), bf16),
            pltpu.VMEM((2 * SEL, n_chan * 16), bf16),
            pltpu.VMEM((2, SEL, LANES), bf16),
            pltpu.VMEM((2 * ROW, SEL, LANES), bf16),
            pltpu.VMEM((SEL, WAVE_BLOCKS * LANES), f32),
            pltpu.VMEM((STATIONS + 1, tiles, LANES), f32),
            pltpu.VMEM((n_chan // HALVES, tiles, LANES), f32),
            pltpu.VMEM((n_chan // HALVES, tiles, LANES), f32),
            pltpu.VMEM((n_chan // HALVES, tiles, LANES), f32),
            pltpu.VMEM((n_chan // HALVES, tiles, LANES), bf16),
            pltpu.VMEM((n_chan // HALVES, tiles, LANES), bf16),
            pltpu.VMEM((8, LANES), f32),
            pltpu.VMEM((n_tm, 8, LANES), f32),
            pltpu.SemaphoreType.DMA((10,)),
            pltpu.SemaphoreType.DMA((2, PAIR_PIECES)),
            pltpu.SemaphoreType.DMA((5,)),
        ],
        compiler_params=pltpu.CompilerParams(
            collective_id=0, has_side_effects=True, vmem_limit_bytes=GRANT
        ),
    )(channel_list, moveouts, seismic, jnp.transpose(waveforms, (1, 0, 2)))
    return stack.reshape(1, piece), jnp.max(peak).reshape(1)


def solution(mesh):
    return jax.shard_map(
        functools.partial(on_device, mesh.shape["chan"], mesh.shape["tm"]),
        mesh=mesh,
        in_specs=(P("chan", "tm"), P("chan", None, None), P(), P()),
        out_specs=(P("chan", "tm"), P("chan")),
        check_vma=False,
    )
```
